32 devices in a mesh: dp: 8 (over z, x), tm: 4 (over y, core).
Axes of the slice: x: 2, y: 2, z: 4, core: 2. Of those that a mesh axis runs over, the one named last changes fastest.
Arguments:
- clip_input: bfloat16 [8, 8, 256, 384], P('dp', 'tm'), may hold values from -32 to 32
- norm_gain: float32 [384], replicated, may hold values from 0.1 to 1.9
- qkv_weight: bfloat16 [384, 1152], replicated, may hold values from -2 to 2
- out_weight: bfloat16 [384, 384], replicated, may hold values from -0.3125 to 0.3125
- time_weight: bfloat16 [3, 384, 768], P(None, 'dp'), may hold values from -0.1875 to 0.1875
- upsample_cotangent: bfloat16 [8, 8, 256, 768], P('dp', 'tm'), may hold values from -6 to 6
Outputs:
- input_grad: bfloat16 [8, 8, 256, 384], P('dp', 'tm')
- qkv_grad: float32 [384, 1152], P('dp', 'tm')
The draws below stay inside these ranges and needn't reach their ends.
All inputs are finite; a program needn't handle non-finite values.
Results may differ from the reference program's by a relative error of at most 0.024.
Values may be sent and summed in bfloat16 or wider, within the bound.
A program may use at most 64 MiB of HBM per device.

```python
import math
import jax
import jax.numpy as jnp
from jax import lax

C = 384
HW = 256
FRAMES = 8
CLIPS = 8
WIDE = 768


def draw_clip_input(key, part):
    own_key = jax.random.fold_in(key, 11)
    pair_key, jitter_key = jax.random.split(own_key, 2)
    block_width = C // CLIPS
    pairing = jax.random.permutation(pair_key, CLIPS)
    channel_block = jnp.arange(C) // block_width
    spiked = 1.0 + 3.0 * (channel_block[None, :] == pairing[:, None]).astype(jnp.float32)
    jitter = jax.random.truncated_normal(jitter_key, -6.0, 6.0, (CLIPS, FRAMES, HW, C), jnp.float32)
    values = jitter * spiked[:, None, None, :]
    return values.astype(jnp.bfloat16)


def draw_qkv_weight(key, part):
    own_key = jax.random.fold_in(key, 23)
    random_key = jax.random.fold_in(own_key, 0)
    spread = C ** (-0.5)
    values = jax.random.truncated_normal(random_key, -6.0, 6.0, (C, 3 * C), jnp.float32) * spread
    return values.astype(jnp.bfloat16)


def steps_of(rng, extent, cuts, least, largest):
    level = 1.0
    for dim, blocks in cuts:
        steps = jax.random.uniform(jax.random.fold_in(jax.random.fold_in(rng, 6), dim), (blocks,), jnp.float32, least / len(cuts), largest / len(cuts))
        level = level * jnp.repeat(jnp.exp(steps), extent[dim] // blocks).reshape((-1,) + (1,) * (len(extent) - 1 - dim))
    return level


def scatter_about(key, shape, scale, bound, cuts=(), held_as=jnp.bfloat16):
    entries = scale * jax.random.normal(key, shape, jnp.float32)
    if cuts:
        entries = entries * steps_of(key, shape, cuts, -0.22, 0.18)
    return jnp.clip(entries, -bound, bound).astype(held_as)


def setup_inputs(seed: int = 0) -> dict:
    key_of = jax.random.split(jax.random.key(seed), 7)
    clip_input = draw_clip_input(jax.random.fold_in(key_of[6], 71), 0)
    norm_gain = jnp.clip(1.0 + 0.18 * jax.random.normal(key_of[1], (C,), jnp.float32), 0.1, 1.9)
    qkv_weight = draw_qkv_weight(jax.random.fold_in(key_of[6], 71), 0)
    out_weight = scatter_about(key_of[3], (C, C), C ** -0.5, 0.3125)
    time_weight = scatter_about(key_of[4], (3, C, WIDE), (3 * C) ** -0.5, 0.1875, ((1, 8),))
    upsample_cotangent = scatter_about(key_of[5], (CLIPS, FRAMES, HW, WIDE), 1.0, 6.0, ((0, 8), (1, 4)))
    return {"clip_input": clip_input, "norm_gain": norm_gain, "qkv_weight": qkv_weight, "out_weight": out_weight, "time_weight": time_weight, "upsample_cotangent": upsample_cotangent}


def rms_scaled(features, norm_gain):
    squares = lax.optimization_barrier(jnp.mean(features * features, axis=-1, keepdims=True))
    return features * lax.rsqrt(squares + 1e-06) * norm_gain

def block_tail(qkv_rows, features, out_weight):
    width = features.shape[-1]
    queries = qkv_rows[..., :width]
    keys = qkv_rows[..., width:2 * width]
    values = qkv_rows[..., 2 * width:]
    scores = jnp.einsum('fqc,fkc->fqk', queries, keys, preferred_element_type=jnp.float32) / math.sqrt(width)
    weights = jax.nn.softmax(scores, axis=-1).astype(jnp.bfloat16)
    mixed = jnp.einsum('fqk,fkc->fqc', weights, values, preferred_element_type=jnp.float32).astype(jnp.bfloat16)
    branch = jnp.einsum('fqc,cd->fqd', mixed, out_weight, preferred_element_type=jnp.float32)
    return (features + branch).astype(jnp.bfloat16)

def attention_grads(clip_rows, norm_gain, qkv_weight, out_weight, upstream):
    features = clip_rows.astype(jnp.float32)
    normed, pre_back = jax.vjp(lambda value: rms_scaled(value, norm_gain), features)
    normed_bf = normed.astype(jnp.bfloat16)
    qkv_rows = jnp.einsum('fhc,cd->fhd', normed_bf, qkv_weight, preferred_element_type=jnp.float32).astype(jnp.bfloat16)
    block_out, tail_back = jax.vjp(lambda first, second: block_tail(first, second, out_weight), qkv_rows, features)
    qkv_cot, feature_cot = tail_back(upstream)
    normed_cot = jnp.einsum('fhd,cd->fhc', qkv_cot, qkv_weight, preferred_element_type=jnp.float32)
    direct = pre_back(normed_cot)[0]
    input_grad = (feature_cot + direct).astype(jnp.bfloat16)
    return (input_grad, normed_bf, qkv_cot)

def reference(clip_input, norm_gain, qkv_weight, out_weight, time_weight, upsample_cotangent):

    def per_clip(total, pair):
        rows, cotangent = pair
        frames = cotangent.shape[0]
        padded = jnp.concatenate([cotangent, jnp.zeros((2,) + cotangent.shape[1:], cotangent.dtype)], 0)
        upstream = jnp.zeros(rows.shape, jnp.float32)
        for tap in range(3):
            upstream = upstream + jnp.einsum('fhd,cd->fhc', padded[2 - tap:2 - tap + frames], time_weight[tap], preferred_element_type=jnp.float32)
        upstream = upstream.astype(jnp.bfloat16)
        input_grad, normed_bf, qkv_cot = attention_grads(rows, norm_gain, qkv_weight, out_weight, upstream)
        term = jnp.einsum('fhc,fhd->cd', normed_bf, qkv_cot, preferred_element_type=jnp.float32)
        return (total + term, input_grad)
    width = clip_input.shape[-1]
    start = jnp.zeros((width, 3 * width), jnp.float32)
    total, grads = lax.scan(per_clip, start, (clip_input, upsample_cotangent))
    return (grads, total)
```

```python
import functools
import math

import jax
import jax.numpy as jnp
from jax import lax
from jax.experimental import pallas as pl
from jax.experimental.pallas import tpu as pltpu
from jax.sharding import PartitionSpec as P


def passed_along(block, axis, distance):
    devices = range(lax.axis_size(axis))
    route = [(i - distance, i) for i in devices if i - distance in devices]
    return lax.ppermute(block, axis, route)


def rms_scaled(features, norm_gain):
    squares = jnp.mean(features * features, axis=-1, keepdims=True)
    return features * lax.rsqrt(squares + 1e-06) * norm_gain


def block_tail(qkv_rows, features, out_weight):
    width = features.shape[-1]
    queries = qkv_rows[..., :width]
    keys = qkv_rows[..., width : 2 * width]
    values = qkv_rows[..., 2 * width :]
    scores = jnp.einsum(
        "fqc,fkc->fqk", queries, keys, preferred_element_type=jnp.float32
    ) / math.sqrt(width)
    weights = jax.nn.softmax(scores, axis=-1).astype(jnp.bfloat16)
    mixed = jnp.einsum("fqk,fkc->fqc", weights, values, preferred_element_type=jnp.float32).astype(
        jnp.bfloat16
    )
    branch = jnp.einsum("fqc,cd->fqd", mixed, out_weight, preferred_element_type=jnp.float32)
    return (features + branch).astype(jnp.bfloat16)


def attention_grads(clip_rows, norm_gain, qkv_weight, out_weight, upstream):
    features = clip_rows.astype(jnp.float32)
    normed, pre_back = jax.vjp(lambda value: rms_scaled(value, norm_gain), features)
    normed_bf = normed.astype(jnp.bfloat16)
    qkv_rows = jnp.einsum(
        "fhc,cd->fhd", normed_bf, qkv_weight, preferred_element_type=jnp.float32
    ).astype(jnp.bfloat16)
    block_out, tail_back = jax.vjp(
        lambda first, second: block_tail(first, second, out_weight), qkv_rows, features
    )
    qkv_cot, feature_cot = tail_back(upstream)
    normed_cot = jnp.einsum("fhd,cd->fhc", qkv_cot, qkv_weight, preferred_element_type=jnp.float32)
    direct = pre_back(normed_cot)[0]
    input_grad = (feature_cot + direct).astype(jnp.bfloat16)
    return (input_grad, normed_bf, qkv_cot)


def on_device_by_collectives(clip_input, norm_gain, qkv_weight, out_weight, time_weight, upsample_cotangent):
    rows = clip_input[0]
    cotangent = upsample_cotangent[0]
    frames = cotangent.shape[0]
    width = rows.shape[-1]
    incoming = passed_along(cotangent, "tm", -1)
    padded = jnp.concatenate([cotangent, incoming], 0)
    piece = lax.all_gather(time_weight, "dp", axis=1, tiled=True)
    result = jnp.einsum(
        "fhd,cd->fhc", padded[2 : 2 + frames], piece[0], preferred_element_type=jnp.float32
    )
    result = result + jnp.einsum(
        "fhd,cd->fhc", padded[1 : 1 + frames], piece[1], preferred_element_type=jnp.float32
    )
    upstream = (
        result
        + jnp.einsum("fhd,cd->fhc", padded[0:frames], piece[2], preferred_element_type=jnp.float32)
    ).astype(jnp.bfloat16)
    input_grad, normed_bf, qkv_cot = attention_grads(
        rows, norm_gain, qkv_weight, out_weight, upstream
    )
    flat_normed = normed_bf.reshape(-1, width)
    flat_cot = qkv_cot.reshape(-1, 3 * width)
    shares = lax.psum_scatter(
        jnp.einsum("rc,rd->cd", flat_normed, flat_cot, preferred_element_type=jnp.float32).astype(
            jnp.bfloat16
        ),
        "dp",
        scatter_dimension=0,
        tiled=True,
    )
    qkv_grad = lax.psum_scatter(shares, "tm", scatter_dimension=1, tiled=True).astype(jnp.float32)
    return (input_grad[None], qkv_grad)


LANES = 128
MESH = pl.DeviceIdType.MESH
F32 = jnp.float32
BF16 = jnp.bfloat16


def matmul(a, b, contract):
    return lax.dot_general(a, b, (contract, ((), ())), preferred_element_type=F32)


PLAIN = ((1,), (0,))
RIGHT_T = ((1,), (1,))
LEFT_T = ((0,), (0,))


def fused_kernel(
    nz,
    clip_hbm,
    gain_ref,
    qkv_w_hbm,
    out_w_hbm,
    taps_hbm,
    cot_hbm,
    grad_in_hbm,
    grad_w_ref,
    clip,
    qkv_w,
    out_w,
    taps,
    cot,
    normed,
    qkv,
    probs,
    upstream,
    qkv_cot,
    grad_in,
    grad,
    core_in,
    y_out,
    y_in,
    kept,
    x_out,
    x_in,
    z_out,
    z_in,
    local_sem,
    cot_send,
    cot_recv,
    z_send,
    line_recv,
    x_send,
    across_recv,
    pair_send,
    pair_recv,
    rs_send,
    rs_recv,
):
    dp, tm = lax.axis_index("dp"), lax.axis_index("tm")
    z, x = dp // 2, dp % 2
    y, core = tm // 2, tm % 2
    frames, hw, width = clip_hbm.shape
    wide = cot_hbm.shape[-1]
    half = wide // 2
    rows = frames * hw
    cols = width * 3 // 4
    window = -(-cols // LANES) * LANES
    stride = cols // LANES * LANES
    scale = 1.0 / math.sqrt(width)
    span = nz - 1

    across = (z * 2 + 1 - x, tm)
    pair = (dp, y * 2 + 1 - core)
    other_y = (dp, (1 - y) * 2 + core)

    def along_z(d):
        return ((z + d) * 2 + x, tm)

    def there(d):
        return jnp.logical_and(z + d >= 0, z + d < nz)

    locals_ = [
        pltpu.make_async_copy(clip_hbm, clip, local_sem.at[0]),
        pltpu.make_async_copy(qkv_w_hbm, qkv_w, local_sem.at[1]),
        pltpu.make_async_copy(taps_hbm, taps.at[dp], local_sem.at[2]),
        pltpu.make_async_copy(cot_hbm, cot.at[pl.ds(0, frames)], local_sem.at[3]),
        pltpu.make_async_copy(out_w_hbm, out_w, local_sem.at[4]),
    ]
    for copy in locals_:
        copy.start()

    barrier = pltpu.get_barrier_semaphore()
    for target in (across, pair, other_y, (dp, 3 - tm)):
        pl.semaphore_signal(barrier, inc=1, device_id=target, device_id_type=MESH)
    for d in range(-span, span + 1):
        if d:
            pl.when(there(d))(
                lambda d=d: pl.semaphore_signal(
                    barrier, inc=1, device_id=along_z(d), device_id_type=MESH
                )
            )
    pl.semaphore_wait(barrier, 4 + span)

    def remote(source, target, send, recv, device):
        return pltpu.make_async_remote_copy(
            src_ref=source,
            dst_ref=target,
            send_sem=send,
            recv_sem=recv,
            device_id=device,
            device_id_type=MESH,
        )

    my_half = pl.ds(pl.multiple_of(core * half, LANES), half)

    def slot(line, d):
        return taps.at[(z + d) * 2 + line, :, :, my_half]

    def held(d):
        return taps_hbm.at[:, :, my_half] if d == 0 else slot(x, d)

    def z_copy(d, step):
        return remote(
            held(d),
            slot(x, d),
            z_send.at[(0 if step > 0 else 1), d + span],
            line_recv.at[d - step + span],
            along_z(step),
        )

    def across_copy(d):
        return remote(held(d), slot(x, d), x_send.at[d + span], across_recv.at[d + span], across)

    def pair_copy(line, d):
        own = 0 if line == "own" else 1
        where = slot(x if own == 0 else 1 - x, d)
        return remote(
            where, where, pair_send.at[own, d + span], pair_recv.at[own, d + span], pair
        )

    def line_wait(d):
        remote(
            slot(x, d), slot(x, d), z_send.at[0, d + span], line_recv.at[d + span], pair
        ).wait_recv()

    def across_wait(d):
        remote(
            slot(1 - x, d), slot(1 - x, d), x_send.at[d + span], across_recv.at[d + span], across
        ).wait_recv()

    pair_incoming = []

    cot_copy = remote(
        cot_hbm, cot.at[pl.ds(frames, frames)], cot_send.at[0], cot_recv.at[0], (dp, tm - 1)
    )

    def start_when(condition, copy):
        pl.when(condition)(lambda: copy().start())

    start_when(tm > 0, lambda: cot_copy)
    start_when(there(1), lambda: z_copy(0, 1))
    start_when(there(-1), lambda: z_copy(0, -1))
    across_copy(0).start()

    def pass_on(d):
        def go():
            line_wait(d)
            step = 1 if d < 0 else -1
            start_when(there(step), lambda: z_copy(d, step))
            across_copy(d).start()
            pair_copy("own", d).start()

        pl.when(there(d))(go)

    def pass_across(d):
        def go():
            across_wait(d)
            pair_copy("other", d).start()

        pl.when(there(d))(go)

    def project():
        locals_[0].wait()
        locals_[1].wait()
        features = clip[...].reshape(rows, width).astype(F32)
        squares = jnp.mean(features * features, axis=-1, keepdims=True)
        normed[...] = (features * lax.rsqrt(squares + 1e-06) * gain_ref[...]).astype(BF16)
        qkv[...] = matmul(normed[...], qkv_w[...], PLAIN).astype(BF16)

    def attend(f):
        at = pl.ds(f * hw, hw)
        scores = matmul(qkv[at, 0:width], qkv[at, width : 2 * width], RIGHT_T) * scale
        weights = jnp.exp(scores - jnp.max(scores, axis=-1, keepdims=True))
        probs[f] = weights / jnp.sum(weights, axis=-1, keepdims=True)

    @pl.when(tm == 3)
    def _():
        cot[frames : 2 * frames] = jnp.zeros((frames, hw, wide), BF16)

    work = [project] + [functools.partial(attend, f) for f in range(frames)]
    for k in range(1, nz):
        if work:
            work.pop(0)()
        pass_on(-k)
        pass_on(k)
        for d in sorted({-(k - 1), k - 1}):
            pass_across(d)
    for step in work:
        step()
    for d in (-span, span):
        pass_across(d)

    locals_[2].wait()
    locals_[3].wait()
    locals_[4].wait()
    pl.when(tm < 3)(lambda: cot_copy.wait_recv())
    pair_half = pl.ds(pl.multiple_of((1 - core) * half, LANES), half)

    def pair_wait(line, own, d):
        where = taps.at[(z + d) * 2 + line, :, :, pair_half]
        remote(
            where, where, pair_send.at[own, d + span], pair_recv.at[own, d + span], pair
        ).wait_recv()

    for d in range(-span, span + 1):
        if d:
            pl.when(there(d))(lambda d=d: pair_wait(x, 0, d))
        pl.when(there(d))(lambda d=d: pair_wait(1 - x, 1, d))

    total = None
    for tap in range(3):
        part = matmul(
            cot[2 - tap : 2 - tap + frames].reshape(rows, wide),
            taps[:, tap].reshape(width, wide),
            RIGHT_T,
        )
        total = part if total is None else total + part
    upstream[...] = total.astype(BF16)
    mixed_cot = matmul(upstream[...], out_w[...], RIGHT_T).astype(BF16)
    for f in range(frames):
        at = pl.ds(f * hw, hw)
        p = probs[f]
        d_mixed = mixed_cot[f * hw : (f + 1) * hw]
        qkv_cot[at, 2 * width : 3 * width] = matmul(p.astype(BF16), d_mixed, LEFT_T).astype(BF16)
        d_weights = matmul(d_mixed, qkv[at, 2 * width : 3 * width], RIGHT_T)
        d_weights = d_weights.astype(BF16).astype(F32)
        inner = jnp.sum(p * d_weights, axis=-1, keepdims=True)
        d_scores = (p * (d_weights - inner) * scale).astype(BF16)
        qkv_cot[at, 0:width] = matmul(d_scores, qkv[at, width : 2 * width], PLAIN).astype(BF16)
        qkv_cot[at, width : 2 * width] = matmul(d_scores, qkv[at, 0:width], LEFT_T).astype(BF16)

    grad[...] = (
        matmul(normed[...], qkv_cot[...], LEFT_T).astype(BF16).reshape(nz, 2, -1, 3 * width)
    )

    def columns(t):
        return pl.ds(pl.multiple_of(t * stride, LANES), window)

    def core_copy(i, side):
        return remote(
            grad.at[:, :, :, columns(side * 2 + 1 - core)],
            core_in.at[i],
            rs_send.at[i],
            rs_recv.at[i],
            pair,
        )

    core_copies = [core_copy(0, 1 - y), core_copy(1, y)]
    for copy in core_copies:
        copy.start()
    y_copies = [
        remote(y_out.at[i], y_in.at[i], rs_send.at[2 + i], rs_recv.at[2 + i], other_y)
        for i in range(2)
    ]
    core_copies[0].wait_recv()
    for i, line in enumerate((1 - x, x)):
        y_out[i] = (
            grad[:, line, :, columns((1 - y) * 2 + core)].astype(F32)
            + core_in[0, :, line].astype(F32)
        ).astype(BF16)
        y_copies[i].start()
    core_copies[1].wait_recv()
    for i, line in enumerate((1 - x, x)):
        kept[i] = grad[:, line, :, columns(tm)].astype(F32) + core_in[1, :, line].astype(F32)

    features = clip[...].reshape(rows, width).astype(F32)
    squares = jnp.mean(features * features, axis=-1, keepdims=True)
    root = lax.rsqrt(squares + 1e-06)
    scaled = matmul(qkv_cot[...], qkv_w[...], RIGHT_T) * gain_ref[...]
    lean = jnp.mean(features * scaled, axis=-1, keepdims=True)
    direct = root * scaled - features * (root * root * root * lean)
    grad_in[...] = (
        (upstream[...].astype(F32) + direct).astype(BF16).reshape(frames, hw, width)
    )
    result_copy = pltpu.make_async_copy(grad_in, grad_in_hbm, local_sem.at[5])
    result_copy.start()

    x_copy = remote(x_out, x_in, rs_send.at[4], rs_recv.at[4], across)
    y_copies[0].wait_recv()
    x_out[...] = (kept[0] + y_in[0].astype(F32)).astype(BF16)
    x_copy.start()
    y_copies[1].wait_recv()
    kept[1] = kept[1] + y_in[1].astype(F32)
    x_copy.wait_recv()
    kept[1] = kept[1] + x_in[...].astype(F32)
    z_out[...] = kept[1].astype(BF16)

    def z_share(d):
        return remote(
            z_out.at[z + d],
            z_in.at[span - d],
            rs_send.at[5 + span + d],
            rs_recv.at[5 + span - d],
            along_z(d),
        )

    def z_wait(d):
        remote(
            z_in.at[span + d],
            z_in.at[span + d],
            rs_send.at[5 + span + d],
            rs_recv.at[5 + span + d],
            along_z(d),
        ).wait_recv()

    distances = [d for k in range(span, 0, -1) for d in (-k, k)]
    for d in distances:
        start_when(there(d), lambda d=d: z_share(d))
    kept[0, 0] = kept[1, z]
    for d in reversed(distances):

        @pl.when(there(d))
        def _(d=d):
            z_wait(d)
            kept[0, 0] = kept[0, 0] + z_in[span + d].astype(F32)

    for t in range(4):

        @pl.when(tm == t)
        def _(t=t):
            first = t * (cols - stride)
            grad_w_ref[...] = kept[0, 0][:, first : first + cols]

    pl.when(tm > 0)(lambda: cot_copy.wait_send())
    across_copy(0).wait_send()
    for step in (1, -1):
        pl.when(there(step))(lambda step=step: z_copy(0, step).wait_send())
    for d in range(-span, span + 1):

        @pl.when(there(d))
        def _(d=d):
            if d:
                step = 1 if d < 0 else -1
                if abs(d) < span:
                    pl.when(there(step))(lambda: z_copy(d, step).wait_send())
                across_copy(d).wait_send()
                pair_copy("own", d).wait_send()
                z_share(d).wait_send()
            pair_copy("other", d).wait_send()

    for copy in core_copies + y_copies + [x_copy]:
        copy.wait_send()
    result_copy.wait()


def on_device(ndp, ntm, clip_input, norm_gain, qkv_weight, out_weight, time_weight, upsample_cotangent):
    _, frames, hw, width = clip_input.shape
    wide = upsample_cotangent.shape[-1]
    share = width // ndp
    fits = ndp % 2 == 0 and ntm == 4 and frames == 2 and share % 16 == 0
    if not fits or width % LANES or wide % (2 * LANES):
        return on_device_by_collectives(
            clip_input, norm_gain, qkv_weight, out_weight, time_weight, upsample_cotangent
        )
    nz = ndp // 2
    cols = 3 * width // ntm
    window = -(-cols // LANES) * LANES
    rows = frames * hw
    steps = 2 * nz - 1
    anywhere = pl.BlockSpec(memory_space=pl.ANY)
    vmem = pl.BlockSpec(memory_space=pltpu.VMEM)
    dma = pltpu.SemaphoreType.DMA
    grad_in, grad_w = pl.pallas_call(
        functools.partial(fused_kernel, nz),
        out_shape=(
            jax.ShapeDtypeStruct((frames, hw, width), BF16),
            jax.ShapeDtypeStruct((share, cols), F32),
        ),
        in_specs=[anywhere, vmem, anywhere, anywhere, anywhere, anywhere],
        out_specs=(anywhere, vmem),
        scratch_shapes=[
            pltpu.VMEM((frames, hw, width), BF16),
            pltpu.VMEM((width, 3 * width), BF16),
            pltpu.VMEM((width, width), BF16),
            pltpu.VMEM((ndp, 3, share, wide), BF16),
            pltpu.VMEM((2 * frames, hw, wide), BF16),
            pltpu.VMEM((rows, width), BF16),
            pltpu.VMEM((rows, 3 * width), BF16),
            pltpu.VMEM((frames, hw, hw), F32),
            pltpu.VMEM((rows, width), BF16),
            pltpu.VMEM((rows, 3 * width), BF16),
            pltpu.VMEM((frames, hw, width), BF16),
            pltpu.VMEM((nz, 2, share, 3 * width), BF16),
            pltpu.VMEM((2, nz, 2, share, window), BF16),
            pltpu.VMEM((2, nz, share, window), BF16),
            pltpu.VMEM((2, nz, share, window), BF16),
            pltpu.VMEM((2, nz, share, window), F32),
            pltpu.VMEM((nz, share, window), BF16),
            pltpu.VMEM((nz, share, window), BF16),
            pltpu.VMEM((nz, share, window), BF16),
            pltpu.VMEM((steps, share, window), BF16),
            dma((6,)),
            dma((1,)),
            dma((1,)),
            dma((2, steps)),
            dma((steps,)),
            dma((steps,)),
            dma((steps,)),
            dma((2, steps)),
            dma((2, steps)),
            dma((5 + steps,)),
            dma((5 + steps,)),
        ],
        compiler_params=pltpu.CompilerParams(
            collective_id=0, has_side_effects=True, vmem_limit_bytes=50 * 1024 * 1024
        ),
        cost_estimate=pl.CostEstimate(
            flops=2 * rows * width * (3 * wide + 10 * width + 6 * hw),
            bytes_accessed=4 * rows * wide + 16 * width * width,
            transcendentals=rows * hw,
        ),
    )(
        clip_input[0],
        norm_gain.reshape(1, width),
        qkv_weight,
        out_weight,
        time_weight,
        upsample_cotangent[0],
    )
    return (grad_in[None], grad_w)


def solution(mesh):
    in_specs = (
        P("dp", "tm", None, None),
        P(),
        P(),
        P(),
        P(None, "dp", None),
        P("dp", "tm", None, None),
    )
    out_specs = (P("dp", "tm", None, None), P("dp", "tm"))
    return jax.shard_map(
        functools.partial(on_device, mesh.shape["dp"], mesh.shape["tm"]),
        mesh=mesh,
        in_specs=in_specs,
        out_specs=out_specs,
        check_vma=False,
    )
```

```python
import functools
import math

import jax
import jax.numpy as jnp
from jax import lax
from jax.experimental import pallas as pl
from jax.experimental.pallas import tpu as pltpu
from jax.sharding import PartitionSpec as P


def passed_along(block, axis, distance):
    devices = range(lax.axis_size(axis))
    route = [(i - distance, i) for i in devices if i - distance in devices]
    return lax.ppermute(block, axis, route)


def rms_scaled(features, norm_gain):
    squares = jnp.mean(features * features, axis=-1, keepdims=True)
    return features * lax.rsqrt(squares + 1e-06) * norm_gain


def block_tail(qkv_rows, features, out_weight):
    width = features.shape[-1]
    queries = qkv_rows[..., :width]
    keys = qkv_rows[..., width : 2 * width]
    values = qkv_rows[..., 2 * width :]
    scores = jnp.einsum(
        "fqc,fkc->fqk", queries, keys, preferred_element_type=jnp.float32
    ) / math.sqrt(width)
    weights = jax.nn.softmax(scores, axis=-1).astype(jnp.bfloat16)
    mixed = jnp.einsum("fqk,fkc->fqc", weights, values, preferred_element_type=jnp.float32).astype(
        jnp.bfloat16
    )
    branch = jnp.einsum("fqc,cd->fqd", mixed, out_weight, preferred_element_type=jnp.float32)
    return (features + branch).astype(jnp.bfloat16)


def attention_grads(clip_rows, norm_gain, qkv_weight, out_weight, upstream):
    features = clip_rows.astype(jnp.float32)
    normed, pre_back = jax.vjp(lambda value: rms_scaled(value, norm_gain), features)
    normed_bf = normed.astype(jnp.bfloat16)
    qkv_rows = jnp.einsum(
        "fhc,cd->fhd", normed_bf, qkv_weight, preferred_element_type=jnp.float32
    ).astype(jnp.bfloat16)
    block_out, tail_back = jax.vjp(
        lambda first, second: block_tail(first, second, out_weight), qkv_rows, features
    )
    qkv_cot, feature_cot = tail_back(upstream)
    normed_cot = jnp.einsum("fhd,cd->fhc", qkv_cot, qkv_weight, preferred_element_type=jnp.float32)
    direct = pre_back(normed_cot)[0]
    input_grad = (feature_cot + direct).astype(jnp.bfloat16)
    return (input_grad, normed_bf, qkv_cot)


def on_device_by_collectives(clip_input, norm_gain, qkv_weight, out_weight, time_weight, upsample_cotangent):
    rows = clip_input[0]
    cotangent = upsample_cotangent[0]
    frames = cotangent.shape[0]
    width = rows.shape[-1]
    incoming = passed_along(cotangent, "tm", -1)
    padded = jnp.concatenate([cotangent, incoming], 0)
    piece = lax.all_gather(time_weight, "dp", axis=1, tiled=True)
    result = jnp.einsum(
        "fhd,cd->fhc", padded[2 : 2 + frames], piece[0], preferred_element_type=jnp.float32
    )
    result = result + jnp.einsum(
        "fhd,cd->fhc", padded[1 : 1 + frames], piece[1], preferred_element_type=jnp.float32
    )
    upstream = (
        result
        + jnp.einsum("fhd,cd->fhc", padded[0:frames], piece[2], preferred_element_type=jnp.float32)
    ).astype(jnp.bfloat16)
    input_grad, normed_bf, qkv_cot = attention_grads(
        rows, norm_gain, qkv_weight, out_weight, upstream
    )
    flat_normed = normed_bf.reshape(-1, width)
    flat_cot = qkv_cot.reshape(-1, 3 * width)
    shares = lax.psum_scatter(
        jnp.einsum("rc,rd->cd", flat_normed, flat_cot, preferred_element_type=jnp.float32).astype(
            jnp.bfloat16
        ),
        "dp",
        scatter_dimension=0,
        tiled=True,
    )
    qkv_grad = lax.psum_scatter(shares, "tm", scatter_dimension=1, tiled=True).astype(jnp.float32)
    return (input_grad[None], qkv_grad)


LANES = 128
VMEM_GRANT = 64 * 1024 * 1024 - 64 * 1024
MESH = pl.DeviceIdType.MESH
F32 = jnp.float32
BF16 = jnp.bfloat16
PLAIN = ((1,), (0,))
RIGHT_T = ((1,), (1,))
LEFT_T = ((0,), (0,))
TAP_ORDER = (2, 1, 0)


def matmul(a, b, contract):
    return lax.dot_general(a, b, (contract, ((), ())), preferred_element_type=F32)


def fused_kernel(
    nz,
    clip_hbm,
    gain_hbm,
    qkv_w_hbm,
    out_w_hbm,
    taps_hbm,
    cot_hbm,
    grad_in_hbm,
    grad_w_hbm,
    clip,
    gain,
    qkv_w,
    out_w,
    taps,
    cot,
    normed,
    normed_t,
    qkv,
    probs,
    weights_t,
    total,
    upstream,
    mixed_cot,
    qkv_cot,
    grad_in,
    grad_w,
    grad,
    pair_in,
    kept,
    x_out,
    x_in,
    z_out,
    z_in,
    slab,
    slab_in,
    local_sem,
    cot_send,
    cot_recv,
    z_send,
    line_recv,
    x_send,
    across_recv,
    pair_send,
    pair_recv,
    rp_send,
    rp_recv,
    rx_send,
    rx_recv,
    rz_send,
    rz_recv,
    rf_send,
    rf_recv,
):
    dp, tm = lax.axis_index("dp"), lax.axis_index("tm")
    z, x = dp // 2, dp % 2
    y, core = tm // 2, tm % 2
    frames, hw, width = clip_hbm.shape
    wide = cot_hbm.shape[-1]
    half = wide // 2
    rows = frames * hw
    cols = width * 3 // 4
    window = -(-cols // LANES) * LANES
    stride = cols // LANES * LANES
    scale = 1.0 / math.sqrt(width)
    span = nz - 1
    zh = nz // 2
    distances = [d for k in range(1, nz) for d in (-k, k)]

    across = (z * 2 + 1 - x, tm)
    pair = (dp, y * 2 + 1 - core)

    def along_z(d):
        return ((z + d) * 2 + x, tm)

    def there(d):
        return jnp.logical_and(z + d >= 0, z + d < nz)

    def remote(source, target, send, recv, device):
        return pltpu.make_async_remote_copy(
            src_ref=source,
            dst_ref=target,
            send_sem=send,
            recv_sem=recv,
            device_id=device,
            device_id_type=MESH,
        )

    def start_when(condition, copy):
        pl.when(condition)(lambda: copy().start())

    locals_ = [
        pltpu.make_async_copy(clip_hbm, clip, local_sem.at[0]),
        pltpu.make_async_copy(qkv_w_hbm, qkv_w, local_sem.at[1]),
        pltpu.make_async_copy(gain_hbm, gain, local_sem.at[6]),
        pltpu.make_async_copy(taps_hbm, taps.at[dp], local_sem.at[2]),
        pltpu.make_async_copy(cot_hbm, cot.at[pl.ds(0, frames)], local_sem.at[3]),
        pltpu.make_async_copy(out_w_hbm, out_w, local_sem.at[4]),
    ]
    barrier = pltpu.get_barrier_semaphore()
    for target in (across, *((dp, (tm + i) % 4) for i in range(1, 4))):
        pl.semaphore_signal(barrier, inc=1, device_id=target, device_id_type=MESH)
    for d in distances:
        pl.when(there(d))(
            lambda d=d: pl.semaphore_signal(
                barrier, inc=1, device_id=along_z(d), device_id_type=MESH
            )
        )
    for copy in locals_:
        copy.start()
    pl.semaphore_wait(barrier, 4 + span)

    my_half = pl.ds(pl.multiple_of(core * half, LANES), half)
    pair_half = pl.ds(pl.multiple_of((1 - core) * half, LANES), half)

    def slot(line, d, tap):
        return taps.at[(z + d) * 2 + line, tap, :, my_half]

    def held(d, tap):
        return taps_hbm.at[tap, :, my_half] if d == 0 else slot(x, d, tap)

    def z_copy(d, step, tap):
        return remote(
            held(d, tap),
            slot(x, d, tap),
            z_send.at[(0 if step > 0 else 1), d + span, tap],
            line_recv.at[d - step + span, tap],
            along_z(step),
        )

    def across_copy(d, tap):
        return remote(
            held(d, tap),
            slot(x, d, tap),
            x_send.at[d + span, tap],
            across_recv.at[d + span, tap],
            across,
        )

    def pair_copy(line, d, tap):
        where = slot(1 - x if line else x, d, tap)
        return remote(
            where, where, pair_send.at[line, d + span, tap], pair_recv.at[line, d + span, tap], pair
        )

    def line_wait(d, tap):
        where = slot(x, d, tap)
        remote(
            where, where, z_send.at[0, d + span, tap], line_recv.at[d + span, tap], pair
        ).wait_recv()

    def across_wait(d, tap):
        where = slot(1 - x, d, tap)
        remote(
            where, where, x_send.at[d + span, tap], across_recv.at[d + span, tap], across
        ).wait_recv()

    def pair_wait(line, d, tap):
        where = taps.at[(z + d) * 2 + (1 - x if line else x), tap, :, pair_half]
        remote(
            where, where, pair_send.at[line, d + span, tap], pair_recv.at[line, d + span, tap], pair
        ).wait_recv()

    def cot_copy(f):
        return remote(cot_hbm.at[f], cot.at[frames + f], cot_send.at[f], cot_recv.at[f], (dp, tm - 1))

    for tap in TAP_ORDER:
        start_when(there(1), lambda: z_copy(0, 1, tap))
        start_when(there(-1), lambda: z_copy(0, -1, tap))
        across_copy(0, tap).start()
    for f in range(frames):
        start_when(tm > 0, lambda: cot_copy(f))

    def pass_on(d, tap):
        @pl.when(there(d))
        def _():
            line_wait(d, tap)
            step = 1 if d < 0 else -1
            start_when(there(step), lambda: z_copy(d, step, tap))
            across_copy(d, tap).start()
            pair_copy(0, d, tap).start()

    def pass_across(d, tap):
        @pl.when(there(d))
        def _():
            across_wait(d, tap)
            pair_copy(1, d, tap).start()

    def project():
        locals_[0].wait()
        locals_[1].wait()
        locals_[2].wait()
        features = clip[...].reshape(rows, width).astype(F32)
        squares = jnp.mean(features * features, axis=-1, keepdims=True)
        normed_bf = (features * lax.rsqrt(squares + 1e-06) * gain[...]).astype(BF16)
        normed[...] = normed_bf
        qkv[...] = matmul(normed_bf, qkv_w[...], PLAIN).astype(BF16)

    def attend(f):
        at = pl.ds(f * hw, hw)
        scores = matmul(qkv[at, 0:width], qkv[at, width : 2 * width], RIGHT_T) * scale
        weights = jnp.exp(scores - jnp.max(scores, axis=-1, keepdims=True))
        weights = weights / jnp.sum(weights, axis=-1, keepdims=True)
        probs[f] = weights
        weights_t[f] = weights.astype(BF16).T

    def turn():
        normed_t[...] = normed[...].T

    @pl.when(tm == 3)
    def _():
        cot[frames : 2 * frames] = jnp.zeros((frames, hw, wide), BF16)

    def gather_step(k, tap):
        pass_on(-k, tap)
        pass_on(k, tap)
        for d in sorted({-(k - 1), k - 1}):
            pass_across(d, tap)

    def gather_end(tap):
        for d in (-span, span):
            pass_across(d, tap)

    def add_tap(tap):
        for d in [0] + distances:
            if d:
                pl.when(there(d))(lambda d=d: pair_wait(0, d, tap))
            pl.when(there(d))(lambda d=d: pair_wait(1, d, tap))
        if tap == TAP_ORDER[0]:
            locals_[3].wait()
            locals_[4].wait()
            locals_[5].wait()
        else:
            pl.when(tm < 3)(lambda: cot_copy(1 - tap).wait_recv())
        part = matmul(
            cot[2 - tap : 2 - tap + frames].reshape(rows, wide),
            taps[:, tap].reshape(width, wide),
            RIGHT_T,
        )
        if tap == TAP_ORDER[0]:
            total[...] = part
        elif tap == TAP_ORDER[-1]:
            upstream[...] = (total[...] + part).astype(BF16)
        else:
            total[...] += part

    work = [project] + [functools.partial(attend, f) for f in range(frames)] + [turn]
    behind = []
    for tap in TAP_ORDER:
        for k in range(1, nz):
            if work:
                work.pop(0)()
            gather_step(k, tap)
        gather_end(tap)
        if behind:
            add_tap(behind.pop())
        behind.append(tap)
    for step in work:
        step()
    add_tap(behind.pop())

    own_z = pl.ds(core * zh, zh)
    owner = z // zh == core

    def rp_copy(g):
        return remote(
            grad.at[g, pl.ds((1 - core) * zh, zh)], pair_in.at[g], rp_send.at[g], rp_recv.at[g], pair
        )

    def rx_copy(g):
        return remote(x_out.at[g], x_in.at[g], rx_send.at[g], rx_recv.at[g], across)

    def rz_copy(g, d):
        return remote(
            z_out.at[g, z + d - core * zh],
            z_in.at[g, span - d],
            rz_send.at[g, span + d],
            rz_recv.at[g, span - d],
            along_z(d),
        )

    def rz_wait(g, d):
        remote(
            z_in.at[g, span + d],
            z_in.at[g, span + d],
            rz_send.at[g, span + d],
            rz_recv.at[g, span + d],
            along_z(d),
        ).wait_recv()

    def to_z(d):
        return jnp.logical_and(there(d), (z + d) // zh == core)

    def reduce_local(g):
        block = qkv_cot[:, g * width : (g + 1) * width]
        grad[g] = matmul(normed_t[...], block, PLAIN).astype(BF16).reshape(nz, 2, -1, width)
        rp_copy(g).start()

    def reduce_x(g):
        rp_copy(g).wait_recv()
        x_out[g] = (
            grad[g, own_z, 1 - x].astype(F32) + pair_in[g, :, 1 - x].astype(F32)
        ).astype(BF16)
        rx_copy(g).start()
        kept[g] = grad[g, own_z, x].astype(F32) + pair_in[g, :, x].astype(F32)

    def reduce_z(g):
        rx_copy(g).wait_recv()
        sums = kept[g] + x_in[g].astype(F32)
        kept[g] = sums
        z_out[g] = sums.astype(BF16)
        for d in reversed(distances):
            start_when(to_z(d), lambda: rz_copy(g, d))

    def reduce_end(g):
        @pl.when(owner)
        def _():
            mine = z - core * zh
            for d in distances:

                @pl.when(there(d))
                def _(d=d):
                    rz_wait(g, d)
                    kept[g, mine] = kept[g, mine] + z_in[g, span + d].astype(F32)

            slab[:, g * width : (g + 1) * width] = kept[g, mine].astype(BF16)

    def columns(t):
        return pl.ds(t * stride, window)

    mixed_cot[...] = matmul(upstream[...], out_w[...], RIGHT_T).astype(BF16)
    for f in range(frames):
        at = pl.ds(f * hw, hw)
        qkv_cot[at, 2 * width : 3 * width] = matmul(weights_t[f], mixed_cot[at, :], PLAIN).astype(
            BF16
        )
    reduce_local(2)
    for f in range(frames):
        at = pl.ds(f * hw, hw)
        p = probs[f]
        d_weights = matmul(mixed_cot[at, :], qkv[at, 2 * width : 3 * width], RIGHT_T)
        d_weights = d_weights.astype(BF16).astype(F32)
        inner = jnp.sum(p * d_weights, axis=-1, keepdims=True)
        d_scores = (p * (d_weights - inner) * scale).astype(BF16)
        qkv_cot[at, 0:width] = matmul(d_scores, qkv[at, width : 2 * width], PLAIN).astype(BF16)
        qkv_cot[at, width : 2 * width] = matmul(d_scores, qkv[at, 0:width], LEFT_T).astype(BF16)
        if f == 0:
            reduce_x(2)
    reduce_local(0)
    reduce_local(1)
    reduce_z(2)
    reduce_x(0)
    reduce_x(1)

    features = clip[...].reshape(rows, width).astype(F32)
    squares = jnp.mean(features * features, axis=-1, keepdims=True)
    root = lax.rsqrt(squares + 1e-06)
    total[...] = matmul(qkv_cot[...], qkv_w[...], RIGHT_T) * gain[...]
    reduce_z(0)
    lean = jnp.mean(features * total[...], axis=-1, keepdims=True)
    direct = root * total[...] - features * (root * root * root * lean)
    grad_in[...] = (upstream[...].astype(F32) + direct).astype(BF16).reshape(frames, hw, width)
    result_copy = pltpu.make_async_copy(grad_in, grad_in_hbm, local_sem.at[5])
    result_copy.start()
    reduce_z(1)
    for g in (2, 0, 1):
        reduce_end(g)

    def slab_copy(t):
        return remote(
            slab.at[:, columns(t)], slab_in.at[y], rf_send.at[t], rf_recv.at[y], (dp, t)
        )

    for t in range(4):
        start_when(jnp.logical_and(owner, tm != t), lambda: slab_copy(t))
    for source in range(2):
        local = jnp.logical_and(owner, y == source)

        @pl.when(local)
        def _():
            at = pl.ds(pl.multiple_of(tm * stride, LANES), window)
            slab_in[source] = slab[:, at]

        @pl.when(jnp.logical_not(local))
        def _():
            remote(
                slab_in.at[source], slab_in.at[source], rf_send.at[0], rf_recv.at[source], pair
            ).wait_recv()

    sums = slab_in[0].astype(F32) + slab_in[1].astype(F32)
    for t in range(4):

        @pl.when(tm == t)
        def _(t=t):
            first = t * (cols - stride)
            grad_w[...] = sums[:, first : first + cols]

    weight_copy = pltpu.make_async_copy(grad_w, grad_w_hbm, local_sem.at[7])
    weight_copy.start()

    for f in range(frames):
        pl.when(tm > 0)(lambda: cot_copy(f).wait_send())
    for tap in TAP_ORDER:
        across_copy(0, tap).wait_send()
        pair_copy(1, 0, tap).wait_send()
        for step in (1, -1):
            pl.when(there(step))(lambda: z_copy(0, step, tap).wait_send())
        for d in distances:

            @pl.when(there(d))
            def _():
                step = 1 if d < 0 else -1
                if abs(d) < span:
                    pl.when(there(step))(lambda: z_copy(d, step, tap).wait_send())
                across_copy(d, tap).wait_send()
                pair_copy(0, d, tap).wait_send()
                pair_copy(1, d, tap).wait_send()

    for g in range(3):
        rp_copy(g).wait_send()
        rx_copy(g).wait_send()
        for d in distances:
            pl.when(to_z(d))(lambda: rz_copy(g, d).wait_send())
    for t in range(4):
        pl.when(jnp.logical_and(owner, tm != t))(lambda: slab_copy(t).wait_send())
    result_copy.wait()
    weight_copy.wait()


def on_device(
    ndp, ntm, clip_input, norm_gain, qkv_weight, out_weight, time_weight, upsample_cotangent
):
    _, frames, hw, width = clip_input.shape
    wide = upsample_cotangent.shape[-1]
    share = width // ndp
    fits = ndp % 4 == 0 and ntm == 4 and frames == 2 and share % 16 == 0
    if not fits or width % LANES or wide % (2 * LANES):
        return on_device_by_collectives(
            clip_input, norm_gain, qkv_weight, out_weight, time_weight, upsample_cotangent
        )
    nz = ndp // 2
    cols = 3 * width // ntm
    window = -(-cols // LANES) * LANES
    rows = frames * hw
    steps = 2 * nz - 1
    anywhere = pl.BlockSpec(memory_space=pl.ANY)
    dma = pltpu.SemaphoreType.DMA
    grad_in, grad_w = pl.pallas_call(
        functools.partial(fused_kernel, nz),
        out_shape=(
            jax.ShapeDtypeStruct((frames, hw, width), BF16),
            jax.ShapeDtypeStruct((share, cols), F32),
        ),
        in_specs=[anywhere] * 6,
        out_specs=(anywhere, anywhere),
        scratch_shapes=[
            pltpu.VMEM((frames, hw, width), BF16),
            pltpu.VMEM((1, width), F32),
            pltpu.VMEM((width, 3 * width), BF16),
            pltpu.VMEM((width, width), BF16),
            pltpu.VMEM((ndp, 3, share, wide), BF16),
            pltpu.VMEM((2 * frames, hw, wide), BF16),
            pltpu.VMEM((rows, width), BF16),
            pltpu.VMEM((width, rows), BF16),
            pltpu.VMEM((rows, 3 * width), BF16),
            pltpu.VMEM((frames, hw, hw), F32),
            pltpu.VMEM((frames, hw, hw), BF16),
            pltpu.VMEM((rows, width), F32),
            pltpu.VMEM((rows, width), BF16),
            pltpu.VMEM((rows, width), BF16),
            pltpu.VMEM((rows, 3 * width), BF16),
            pltpu.VMEM((frames, hw, width), BF16),
            pltpu.VMEM((share, cols), F32),
            pltpu.VMEM((3, nz, 2, share, width), BF16),
            pltpu.VMEM((3, nz // 2, 2, share, width), BF16),
            pltpu.VMEM((3, nz // 2, share, width), F32),
            pltpu.VMEM((3, nz // 2, share, width), BF16),
            pltpu.VMEM((3, nz // 2, share, width), BF16),
            pltpu.VMEM((3, nz // 2, share, width), BF16),
            pltpu.VMEM((3, steps, share, width), BF16),
            pltpu.VMEM((share, 3 * width), BF16),
            pltpu.VMEM((2, share, window), BF16),
            dma((8,)),
            dma((2,)),
            dma((2,)),
            dma((2, steps, 3)),
            dma((steps, 3)),
            dma((steps, 3)),
            dma((steps, 3)),
            dma((2, steps, 3)),
            dma((2, steps, 3)),
            dma((3,)),
            dma((3,)),
            dma((3,)),
            dma((3,)),
            dma((3, steps)),
            dma((3, steps)),
            dma((4,)),
            dma((2,)),
        ],
        compiler_params=pltpu.CompilerParams(
            collective_id=0, has_side_effects=True, vmem_limit_bytes=VMEM_GRANT
        ),
        cost_estimate=pl.CostEstimate(
            flops=2 * rows * width * (3 * wide + 10 * width + 6 * hw),
            bytes_accessed=4 * rows * wide + 16 * width * width,
            transcendentals=rows * hw,
        ),
    )(
        clip_input[0],
        norm_gain.reshape(1, width),
        qkv_weight,
        out_weight,
        time_weight,
        upsample_cotangent[0],
    )
    return (grad_in[None], grad_w)


def solution(mesh):
    in_specs = (
        P("dp", "tm", None, None),
        P(),
        P(),
        P(),
        P(None, "dp", None),
        P("dp", "tm", None, None),
    )
    out_specs = (P("dp", "tm", None, None), P("dp", "tm"))
    return jax.shard_map(
        functools.partial(on_device, mesh.shape["dp"], mesh.shape["tm"]),
        mesh=mesh,
        in_specs=in_specs,
        out_specs=out_specs,
        check_vma=False,
    )
```

```python
import functools
import math

import jax
import jax.numpy as jnp
from jax import lax
from jax.experimental import pallas as pl
from jax.experimental.pallas import tpu as pltpu
from jax.sharding import PartitionSpec as P


def passed_along(block, axis, distance):
    devices = range(lax.axis_size(axis))
    route = [(i - distance, i) for i in devices if i - distance in devices]
    return lax.ppermute(block, axis, route)


def rms_scaled(features, norm_gain):
    squares = jnp.mean(features * features, axis=-1, keepdims=True)
    return features * lax.rsqrt(squares + 1e-06) * norm_gain


def block_tail(qkv_rows, features, out_weight):
    width = features.shape[-1]
    queries = qkv_rows[..., :width]
    keys = qkv_rows[..., width : 2 * width]
    values = qkv_rows[..., 2 * width :]
    scores = jnp.einsum(
        "fqc,fkc->fqk", queries, keys, preferred_element_type=jnp.float32
    ) / math.sqrt(width)
    weights = jax.nn.softmax(scores, axis=-1).astype(jnp.bfloat16)
    mixed = jnp.einsum("fqk,fkc->fqc", weights, values, preferred_element_type=jnp.float32).astype(
        jnp.bfloat16
    )
    branch = jnp.einsum("fqc,cd->fqd", mixed, out_weight, preferred_element_type=jnp.float32)
    return (features + branch).astype(jnp.bfloat16)


def attention_grads(clip_rows, norm_gain, qkv_weight, out_weight, upstream):
    features = clip_rows.astype(jnp.float32)
    normed, pre_back = jax.vjp(lambda value: rms_scaled(value, norm_gain), features)
    normed_bf = normed.astype(jnp.bfloat16)
    qkv_rows = jnp.einsum(
        "fhc,cd->fhd", normed_bf, qkv_weight, preferred_element_type=jnp.float32
    ).astype(jnp.bfloat16)
    block_out, tail_back = jax.vjp(
        lambda first, second: block_tail(first, second, out_weight), qkv_rows, features
    )
    qkv_cot, feature_cot = tail_back(upstream)
    normed_cot = jnp.einsum("fhd,cd->fhc", qkv_cot, qkv_weight, preferred_element_type=jnp.float32)
    direct = pre_back(normed_cot)[0]
    input_grad = (feature_cot + direct).astype(jnp.bfloat16)
    return (input_grad, normed_bf, qkv_cot)


def on_device_by_collectives(clip_input, norm_gain, qkv_weight, out_weight, time_weight, upsample_cotangent):
    rows = clip_input[0]
    cotangent = upsample_cotangent[0]
    frames = cotangent.shape[0]
    width = rows.shape[-1]
    incoming = passed_along(cotangent, "tm", -1)
    padded = jnp.concatenate([cotangent, incoming], 0)
    piece = lax.all_gather(time_weight, "dp", axis=1, tiled=True)
    result = jnp.einsum(
        "fhd,cd->fhc", padded[2 : 2 + frames], piece[0], preferred_element_type=jnp.float32
    )
    result = result + jnp.einsum(
        "fhd,cd->fhc", padded[1 : 1 + frames], piece[1], preferred_element_type=jnp.float32
    )
    upstream = (
        result
        + jnp.einsum("fhd,cd->fhc", padded[0:frames], piece[2], preferred_element_type=jnp.float32)
    ).astype(jnp.bfloat16)
    input_grad, normed_bf, qkv_cot = attention_grads(
        rows, norm_gain, qkv_weight, out_weight, upstream
    )
    flat_normed = normed_bf.reshape(-1, width)
    flat_cot = qkv_cot.reshape(-1, 3 * width)
    shares = lax.psum_scatter(
        jnp.einsum("rc,rd->cd", flat_normed, flat_cot, preferred_element_type=jnp.float32).astype(
            jnp.bfloat16
        ),
        "dp",
        scatter_dimension=0,
        tiled=True,
    )
    qkv_grad = lax.psum_scatter(shares, "tm", scatter_dimension=1, tiled=True).astype(jnp.float32)
    return (input_grad[None], qkv_grad)


LANES = 128
VMEM_GRANT = 64 * 1024 * 1024 - 64 * 1024
MESH = pl.DeviceIdType.MESH
F32 = jnp.float32
BF16 = jnp.bfloat16
PLAIN = ((1,), (0,))
RIGHT_T = ((1,), (1,))
LEFT_T = ((0,), (0,))
CHUNKS = ((2, 1), (0, 2))


def matmul(a, b, contract):
    return lax.dot_general(a, b, (contract, ((), ())), preferred_element_type=F32)


def fused_kernel(
    nz,
    clip_hbm,
    gain_hbm,
    qkv_w_hbm,
    out_w_hbm,
    taps_hbm,
    cot_hbm,
    grad_in_hbm,
    grad_w_hbm,
    clip,
    gain,
    qkv_w,
    out_w,
    taps,
    cot,
    normed,
    normed_t,
    qkv,
    probs,
    weights_t,
    total,
    upstream,
    mixed_cot,
    qkv_cot,
    grad_in,
    grad_w,
    grad,
    pair_in,
    kept,
    x_out,
    x_in,
    z_out,
    z_in,
    slab,
    slab_in,
    local_sem,
    cot_send,
    cot_recv,
    z_send,
    line_recv,
    x_send,
    across_recv,
    pair_send,
    pair_recv,
    rp_send,
    rp_recv,
    rx_send,
    rx_recv,
    rz_send,
    rz_recv,
    rf_send,
    rf_recv,
):
    dp, tm = lax.axis_index("dp"), lax.axis_index("tm")
    z, x = dp // 2, dp % 2
    y, core = tm // 2, tm % 2
    frames, hw, width = clip_hbm.shape
    wide = cot_hbm.shape[-1]
    half = wide // 2
    rows = frames * hw
    cols = width * 3 // 4
    window = -(-cols // LANES) * LANES
    stride = cols // LANES * LANES
    scale = 1.0 / math.sqrt(width)
    span = nz - 1
    zh = nz // 2
    distances = [d for k in range(1, nz) for d in (-k, k)]

    across = (z * 2 + 1 - x, tm)
    pair = (dp, y * 2 + 1 - core)

    def along_z(d):
        return ((z + d) * 2 + x, tm)

    def there(d):
        return jnp.logical_and(z + d >= 0, z + d < nz)

    def remote(source, target, send, recv, device):
        return pltpu.make_async_remote_copy(
            src_ref=source,
            dst_ref=target,
            send_sem=send,
            recv_sem=recv,
            device_id=device,
            device_id_type=MESH,
        )

    def start_when(condition, copy):
        pl.when(condition)(lambda: copy().start())

    locals_ = [
        pltpu.make_async_copy(clip_hbm, clip, local_sem.at[0]),
        pltpu.make_async_copy(qkv_w_hbm, qkv_w, local_sem.at[1]),
        pltpu.make_async_copy(gain_hbm, gain, local_sem.at[6]),
        pltpu.make_async_copy(taps_hbm, taps.at[dp], local_sem.at[2]),
        pltpu.make_async_copy(cot_hbm, cot.at[pl.ds(0, frames)], local_sem.at[3]),
        pltpu.make_async_copy(out_w_hbm, out_w, local_sem.at[4]),
    ]
    barrier = pltpu.get_barrier_semaphore()
    for target in (across, *((dp, (tm + i) % 4) for i in range(1, 4))):
        pl.semaphore_signal(barrier, inc=1, device_id=target, device_id_type=MESH)
    for d in distances:
        pl.when(there(d))(
            lambda d=d: pl.semaphore_signal(
                barrier, inc=1, device_id=along_z(d), device_id_type=MESH
            )
        )
    for copy in locals_:
        copy.start()
    pl.semaphore_wait(barrier, 4 + span)

    my_half = pl.ds(pl.multiple_of(core * half, LANES), half)
    pair_half = pl.ds(pl.multiple_of((1 - core) * half, LANES), half)

    def part(c):
        return pl.ds(*CHUNKS[c])

    def slot(line, d, c):
        return taps.at[(z + d) * 2 + line, part(c), :, my_half]

    def held(d, c):
        return taps_hbm.at[part(c), :, my_half] if d == 0 else slot(x, d, c)

    def z_copy(d, c):
        return remote(
            held(0, c),
            slot(x, 0, c),
            z_send.at[d + span, c],
            line_recv.at[span - d, c],
            along_z(d),
        )

    def across_copy(d, c):
        return remote(
            held(d, c), slot(x, d, c), x_send.at[d + span, c], across_recv.at[d + span, c], across
        )

    def pair_copy(line, d, c):
        where = slot(1 - x if line else x, d, c)
        return remote(
            where, where, pair_send.at[line, d + span, c], pair_recv.at[line, d + span, c], pair
        )

    def line_wait(d, c):
        where = slot(x, d, c)
        remote(where, where, z_send.at[d + span, c], line_recv.at[d + span, c], pair).wait_recv()

    def across_wait(d, c):
        where = slot(1 - x, d, c)
        remote(
            where, where, x_send.at[d + span, c], across_recv.at[d + span, c], across
        ).wait_recv()

    def pair_wait(line, d, c):
        where = taps.at[(z + d) * 2 + (1 - x if line else x), part(c), :, pair_half]
        remote(
            where, where, pair_send.at[line, d + span, c], pair_recv.at[line, d + span, c], pair
        ).wait_recv()

    def cot_copy(f):
        return remote(cot_hbm.at[f], cot.at[frames + f], cot_send.at[f], cot_recv.at[f], (dp, tm - 1))

    for c in range(len(CHUNKS)):
        across_copy(0, c).start()
        for d in distances:
            start_when(there(d), lambda: z_copy(d, c))
    for f in range(frames):
        start_when(tm > 0, lambda: cot_copy(f))

    def pass_on(d, c):
        @pl.when(there(d))
        def _():
            line_wait(d, c)
            across_copy(d, c).start()
            pair_copy(0, d, c).start()

    def pass_across(d, c):
        @pl.when(there(d))
        def _():
            across_wait(d, c)
            pair_copy(1, d, c).start()

    def project():
        locals_[0].wait()
        locals_[1].wait()
        locals_[2].wait()
        features = clip[...].reshape(rows, width).astype(F32)
        squares = jnp.mean(features * features, axis=-1, keepdims=True)
        normed_bf = (features * lax.rsqrt(squares + 1e-06) * gain[...].reshape(1, width)).astype(BF16)
        normed[...] = normed_bf
        qkv[...] = matmul(normed_bf, qkv_w[...], PLAIN).astype(BF16)

    def attend(f):
        at = pl.ds(f * hw, hw)
        scores = matmul(qkv[at, 0:width], qkv[at, width : 2 * width], RIGHT_T) * scale
        weights = jnp.exp(scores - jnp.max(scores, axis=-1, keepdims=True))
        weights = weights / jnp.sum(weights, axis=-1, keepdims=True)
        probs[f] = weights
        weights_t[f] = weights.astype(BF16).T

    def turn():
        normed_t[...] = normed[...].T

    @pl.when(tm == 3)
    def _():
        cot[frames : 2 * frames] = jnp.zeros((frames, hw, wide), BF16)

    def add_taps(c):
        for d in [0] + distances:
            if d:
                pl.when(there(d))(lambda: pair_wait(0, d, c))
            pl.when(there(d))(lambda: pair_wait(1, d, c))
        if c == 0:
            locals_[3].wait()
            locals_[4].wait()
            locals_[5].wait()
        else:
            for f in range(frames):
                pl.when(tm < 3)(lambda: cot_copy(f).wait_recv())
        first, count = CHUNKS[c]
        added = None
        for tap in range(first, first + count):
            term = matmul(
                cot[2 - tap : 2 - tap + frames].reshape(rows, wide),
                taps[:, tap].reshape(width, wide),
                RIGHT_T,
            )
            added = term if added is None else added + term
        if c == 0:
            total[...] = added
        else:
            upstream[...] = (total[...] + added).astype(BF16)

    project()
    pass_on(-1, 0)
    pass_on(1, 0)
    attend(0)
    for d in distances[2:]:
        pass_on(d, 0)
    attend(1)
    pass_across(0, 0)
    for d in distances:
        pass_on(d, 1)
    turn()
    for d in distances:
        pass_across(d, 0)
    add_taps(0)
    for d in [0] + distances:
        pass_across(d, 1)
    add_taps(1)

    own_z = pl.ds(core * zh, zh)
    owner = z // zh == core

    def rp_copy(g):
        return remote(
            grad.at[g, pl.ds((1 - core) * zh, zh)], pair_in.at[g], rp_send.at[g], rp_recv.at[g], pair
        )

    def rx_copy(g):
        return remote(x_out.at[g], x_in.at[g], rx_send.at[g], rx_recv.at[g], across)

    def rz_copy(g, d):
        return remote(
            z_out.at[g, z + d - core * zh],
            z_in.at[g, span - d],
            rz_send.at[g, span + d],
            rz_recv.at[g, span - d],
            along_z(d),
        )

    def rz_wait(g, d):
        remote(
            z_in.at[g, span + d],
            z_in.at[g, span + d],
            rz_send.at[g, span + d],
            rz_recv.at[g, span + d],
            along_z(d),
        ).wait_recv()

    def to_z(d):
        return jnp.logical_and(there(d), (z + d) // zh == core)

    def reduce_local(g):
        block = qkv_cot[:, g * width : (g + 1) * width]
        grad[g] = matmul(normed_t[...], block, PLAIN).astype(BF16).reshape(nz, 2, -1, width)
        rp_copy(g).start()

    def reduce_x(g):
        rp_copy(g).wait_recv()
        x_out[g] = (
            grad[g, own_z, 1 - x].astype(F32) + pair_in[g, :, 1 - x].astype(F32)
        ).astype(BF16)
        rx_copy(g).start()
        kept[g] = grad[g, own_z, x].astype(F32) + pair_in[g, :, x].astype(F32)

    def reduce_z(g):
        rx_copy(g).wait_recv()
        sums = kept[g] + x_in[g].astype(F32)
        kept[g] = sums
        z_out[g] = sums.astype(BF16)
        for d in reversed(distances):
            start_when(to_z(d), lambda: rz_copy(g, d))

    def reduce_end(g):
        @pl.when(owner)
        def _():
            mine = z - core * zh
            for d in distances:

                @pl.when(there(d))
                def _(d=d):
                    rz_wait(g, d)
                    kept[g, mine] = kept[g, mine] + z_in[g, span + d].astype(F32)

            slab[:, g * width : (g + 1) * width] = kept[g, mine].astype(BF16)

    def columns(t):
        return pl.ds(t * stride, window)

    mixed_cot[...] = matmul(upstream[...], out_w[...], RIGHT_T).astype(BF16)
    for f in range(frames):
        at = pl.ds(f * hw, hw)
        qkv_cot[at, 2 * width : 3 * width] = matmul(weights_t[f], mixed_cot[at, :], PLAIN).astype(
            BF16
        )
    reduce_local(2)
    for f in range(frames):
        at = pl.ds(f * hw, hw)
        p = probs[f]
        d_weights = matmul(mixed_cot[at, :], qkv[at, 2 * width : 3 * width], RIGHT_T)
        d_weights = d_weights.astype(BF16).astype(F32)
        inner = jnp.sum(p * d_weights, axis=-1, keepdims=True)
        d_scores = (p * (d_weights - inner) * scale).astype(BF16)
        qkv_cot[at, 0:width] = matmul(d_scores, qkv[at, width : 2 * width], PLAIN).astype(BF16)
        qkv_cot[at, width : 2 * width] = matmul(d_scores, qkv[at, 0:width], LEFT_T).astype(BF16)
        if f == 0:
            reduce_x(2)
    reduce_local(0)
    reduce_local(1)
    reduce_z(2)
    reduce_x(0)
    reduce_x(1)

    features = clip[...].reshape(rows, width).astype(F32)
    squares = jnp.mean(features * features, axis=-1, keepdims=True)
    root = lax.rsqrt(squares + 1e-06)
    total[...] = matmul(qkv_cot[...], qkv_w[...], RIGHT_T) * gain[...].reshape(1, width)
    reduce_z(0)
    lean = jnp.mean(features * total[...], axis=-1, keepdims=True)
    direct = root * total[...] - features * (root * root * root * lean)
    grad_in[...] = (upstream[...].astype(F32) + direct).astype(BF16).reshape(frames, hw, width)
    result_copy = pltpu.make_async_copy(grad_in, grad_in_hbm, local_sem.at[5])
    result_copy.start()
    reduce_z(1)
    for f in range(frames):
        pl.when(tm > 0)(lambda: cot_copy(f).wait_send())
    for c in range(len(CHUNKS)):
        across_copy(0, c).wait_send()
        pair_copy(1, 0, c).wait_send()
        for d in distances:

            @pl.when(there(d))
            def _():
                z_copy(d, c).wait_send()
                across_copy(d, c).wait_send()
                pair_copy(0, d, c).wait_send()
                pair_copy(1, d, c).wait_send()

    for g in (2, 0, 1):
        reduce_end(g)

    def slab_copy(t):
        return remote(
            slab.at[:, columns(t)], slab_in.at[y], rf_send.at[t], rf_recv.at[y], (dp, t)
        )

    for t in range(4):
        start_when(jnp.logical_and(owner, tm != t), lambda: slab_copy(t))
    for source in range(2):
        local = jnp.logical_and(owner, y == source)

        @pl.when(local)
        def _():
            at = pl.ds(pl.multiple_of(tm * stride, LANES), window)
            slab_in[source] = slab[:, at]

        @pl.when(jnp.logical_not(local))
        def _():
            remote(
                slab_in.at[source], slab_in.at[source], rf_send.at[0], rf_recv.at[source], pair
            ).wait_recv()

    sums = slab_in[0].astype(F32) + slab_in[1].astype(F32)
    for t in range(4):

        @pl.when(tm == t)
        def _(t=t):
            first = t * (cols - stride)
            grad_w[...] = sums[:, first : first + cols]

    weight_copy = pltpu.make_async_copy(grad_w, grad_w_hbm, local_sem.at[7])
    weight_copy.start()

    for g in range(3):
        rp_copy(g).wait_send()
        rx_copy(g).wait_send()
        for d in distances:
            pl.when(to_z(d))(lambda: rz_copy(g, d).wait_send())
    for t in range(4):
        pl.when(jnp.logical_and(owner, tm != t))(lambda: slab_copy(t).wait_send())
    result_copy.wait()
    weight_copy.wait()


def on_device(
    ndp, ntm, clip_input, norm_gain, qkv_weight, out_weight, time_weight, upsample_cotangent
):
    _, frames, hw, width = clip_input.shape
    wide = upsample_cotangent.shape[-1]
    share = width // ndp
    fits = ndp % 4 == 0 and ntm == 4 and frames == 2 and share % 16 == 0
    if not fits or width % LANES or wide % (2 * LANES):
        return on_device_by_collectives(
            clip_input, norm_gain, qkv_weight, out_weight, time_weight, upsample_cotangent
        )
    nz = ndp // 2
    cols = 3 * width // ntm
    window = -(-cols // LANES) * LANES
    rows = frames * hw
    steps = 2 * nz - 1
    chunks = len(CHUNKS)
    anywhere = pl.BlockSpec(memory_space=pl.ANY)
    dma = pltpu.SemaphoreType.DMA
    grad_in, grad_w = pl.pallas_call(
        functools.partial(fused_kernel, nz),
        out_shape=(
            jax.ShapeDtypeStruct((frames, hw, width), BF16),
            jax.ShapeDtypeStruct((share, cols), F32),
        ),
        in_specs=[anywhere] * 6,
        out_specs=(anywhere, anywhere),
        scratch_shapes=[
            pltpu.VMEM((frames, hw, width), BF16),
            pltpu.VMEM((width,), F32),
            pltpu.VMEM((width, 3 * width), BF16),
            pltpu.VMEM((width, width), BF16),
            pltpu.VMEM((ndp, 3, share, wide), BF16),
            pltpu.VMEM((2 * frames, hw, wide), BF16),
            pltpu.VMEM((rows, width), BF16),
            pltpu.VMEM((width, rows), BF16),
            pltpu.VMEM((rows, 3 * width), BF16),
            pltpu.VMEM((frames, hw, hw), F32),
            pltpu.VMEM((frames, hw, hw), BF16),
            pltpu.VMEM((rows, width), F32),
            pltpu.VMEM((rows, width), BF16),
            pltpu.VMEM((rows, width), BF16),
            pltpu.VMEM((rows, 3 * width), BF16),
            pltpu.VMEM((frames, hw, width), BF16),
            pltpu.VMEM((share, cols), F32),
            pltpu.VMEM((3, nz, 2, share, width), BF16),
            pltpu.VMEM((3, nz // 2, 2, share, width), BF16),
            pltpu.VMEM((3, nz // 2, share, width), F32),
            pltpu.VMEM((3, nz // 2, share, width), BF16),
            pltpu.VMEM((3, nz // 2, share, width), BF16),
            pltpu.VMEM((3, nz // 2, share, width), BF16),
            pltpu.VMEM((3, steps, share, width), BF16),
            pltpu.VMEM((share, 3 * width), BF16),
            pltpu.VMEM((2, share, window), BF16),
            dma((8,)),
            dma((2,)),
            dma((2,)),
            dma((steps, chunks)),
            dma((steps, chunks)),
            dma((steps, chunks)),
            dma((steps, chunks)),
            dma((2, steps, chunks)),
            dma((2, steps, chunks)),
            dma((3,)),
            dma((3,)),
            dma((3,)),
            dma((3,)),
            dma((3, steps)),
            dma((3, steps)),
            dma((4,)),
            dma((2,)),
        ],
        compiler_params=pltpu.CompilerParams(
            collective_id=0, has_side_effects=True, vmem_limit_bytes=VMEM_GRANT
        ),
        cost_estimate=pl.CostEstimate(
            flops=2 * rows * width * (3 * wide + 10 * width + 6 * hw),
            bytes_accessed=4 * rows * wide + 16 * width * width,
            transcendentals=rows * hw,
        ),
    )(
        clip_input[0],
        norm_gain,
        qkv_weight,
        out_weight,
        time_weight,
        upsample_cotangent[0],
    )
    return (grad_in[None], grad_w)


def solution(mesh):
    in_specs = (
        P("dp", "tm", None, None),
        P(),
        P(),
        P(),
        P(None, "dp", None),
        P("dp", "tm", None, None),
    )
    out_specs = (P("dp", "tm", None, None), P("dp", "tm"))
    return jax.shard_map(
        functools.partial(on_device, mesh.shape["dp"], mesh.shape["tm"]),
        mesh=mesh,
        in_specs=in_specs,
        out_specs=out_specs,
        check_vma=False,
    )
```

```python
import functools
import math

import jax
import jax.numpy as jnp
from jax import lax
from jax.experimental import pallas as pl
from jax.experimental.pallas import tpu as pltpu
from jax.sharding import PartitionSpec as P


def passed_along(block, axis, distance):
    devices = range(lax.axis_size(axis))
    route = [(i - distance, i) for i in devices if i - distance in devices]
    return lax.ppermute(block, axis, route)


def rms_scaled(features, norm_gain):
    squares = jnp.mean(features * features, axis=-1, keepdims=True)
    return features * lax.rsqrt(squares + 1e-06) * norm_gain


def block_tail(qkv_rows, features, out_weight):
    width = features.shape[-1]
    queries = qkv_rows[..., :width]
    keys = qkv_rows[..., width : 2 * width]
    values = qkv_rows[..., 2 * width :]
    scores = jnp.einsum(
        "fqc,fkc->fqk", queries, keys, preferred_element_type=jnp.float32
    ) / math.sqrt(width)
    weights = jax.nn.softmax(scores, axis=-1).astype(jnp.bfloat16)
    mixed = jnp.einsum("fqk,fkc->fqc", weights, values, preferred_element_type=jnp.float32).astype(
        jnp.bfloat16
    )
    branch = jnp.einsum("fqc,cd->fqd", mixed, out_weight, preferred_element_type=jnp.float32)
    return (features + branch).astype(jnp.bfloat16)


def attention_grads(clip_rows, norm_gain, qkv_weight, out_weight, upstream):
    features = clip_rows.astype(jnp.float32)
    normed, pre_back = jax.vjp(lambda value: rms_scaled(value, norm_gain), features)
    normed_bf = normed.astype(jnp.bfloat16)
    qkv_rows = jnp.einsum(
        "fhc,cd->fhd", normed_bf, qkv_weight, preferred_element_type=jnp.float32
    ).astype(jnp.bfloat16)
    block_out, tail_back = jax.vjp(
        lambda first, second: block_tail(first, second, out_weight), qkv_rows, features
    )
    qkv_cot, feature_cot = tail_back(upstream)
    normed_cot = jnp.einsum("fhd,cd->fhc", qkv_cot, qkv_weight, preferred_element_type=jnp.float32)
    direct = pre_back(normed_cot)[0]
    input_grad = (feature_cot + direct).astype(jnp.bfloat16)
    return (input_grad, normed_bf, qkv_cot)


def on_device_by_collectives(clip_input, norm_gain, qkv_weight, out_weight, time_weight, upsample_cotangent):
    rows = clip_input[0]
    cotangent = upsample_cotangent[0]
    frames = cotangent.shape[0]
    width = rows.shape[-1]
    incoming = passed_along(cotangent, "tm", -1)
    padded = jnp.concatenate([cotangent, incoming], 0)
    piece = lax.all_gather(time_weight, "dp", axis=1, tiled=True)
    result = jnp.einsum(
        "fhd,cd->fhc", padded[2 : 2 + frames], piece[0], preferred_element_type=jnp.float32
    )
    result = result + jnp.einsum(
        "fhd,cd->fhc", padded[1 : 1 + frames], piece[1], preferred_element_type=jnp.float32
    )
    upstream = (
        result
        + jnp.einsum("fhd,cd->fhc", padded[0:frames], piece[2], preferred_element_type=jnp.float32)
    ).astype(jnp.bfloat16)
    input_grad, normed_bf, qkv_cot = attention_grads(
        rows, norm_gain, qkv_weight, out_weight, upstream
    )
    flat_normed = normed_bf.reshape(-1, width)
    flat_cot = qkv_cot.reshape(-1, 3 * width)
    shares = lax.psum_scatter(
        jnp.einsum("rc,rd->cd", flat_normed, flat_cot, preferred_element_type=jnp.float32).astype(
            jnp.bfloat16
        ),
        "dp",
        scatter_dimension=0,
        tiled=True,
    )
    qkv_grad = lax.psum_scatter(shares, "tm", scatter_dimension=1, tiled=True).astype(jnp.float32)
    return (input_grad[None], qkv_grad)


LANES = 128
VMEM_GRANT = 64 * 1024 * 1024 - 64 * 1024
MESH = pl.DeviceIdType.MESH
F32 = jnp.float32
BF16 = jnp.bfloat16
PLAIN = ((1,), (0,))
RIGHT_T = ((1,), (1,))
LEFT_T = ((0,), (0,))


def matmul(a, b, contract):
    return lax.dot_general(a, b, (contract, ((), ())), preferred_element_type=F32)


def fused_kernel(
    nz,
    clip_hbm,
    gain_hbm,
    qkv_w_hbm,
    out_w_hbm,
    taps_hbm,
    cot_hbm,
    grad_in_hbm,
    grad_w_hbm,
    clip,
    gain,
    qkv_w,
    out_w,
    taps,
    cot,
    normed,
    normed_t,
    qkv,
    probs,
    weights_t,
    total,
    upstream,
    mixed_cot,
    qkv_cot,
    grad_in,
    grad_w,
    grad,
    pair_in,
    kept,
    x_out,
    x_in,
    z_out,
    z_in,
    slab,
    slab_in,
    local_sem,
    cot_send,
    cot_recv,
    z_send,
    line_recv,
    x_send,
    across_recv,
    pair_send,
    pair_recv,
    rp_send,
    rp_recv,
    rx_send,
    rx_recv,
    rz_send,
    rz_recv,
    rf_send,
    rf_recv,
):
    dp, tm = lax.axis_index("dp"), lax.axis_index("tm")
    z, x = dp // 2, dp % 2
    y, core = tm // 2, tm % 2
    frames, hw, width = clip_hbm.shape
    wide = cot_hbm.shape[-1]
    half = wide // 2
    rows = frames * hw
    cols = width * 3 // 4
    window = -(-cols // LANES) * LANES
    stride = cols // LANES * LANES
    scale = 1.0 / math.sqrt(width)
    span = nz - 1
    zh = nz // 2
    distances = [d for k in range(1, nz) for d in (-k, k)]

    across = (z * 2 + 1 - x, tm)
    pair = (dp, y * 2 + 1 - core)

    def along_z(d):
        return ((z + d) * 2 + x, tm)

    def there(d):
        return jnp.logical_and(z + d >= 0, z + d < nz)

    def remote(source, target, send, recv, device):
        return pltpu.make_async_remote_copy(
            src_ref=source,
            dst_ref=target,
            send_sem=send,
            recv_sem=recv,
            device_id=device,
            device_id_type=MESH,
        )

    def start_when(condition, copy):
        pl.when(condition)(lambda: copy().start())

    locals_ = [
        pltpu.make_async_copy(clip_hbm, clip, local_sem.at[0]),
        pltpu.make_async_copy(qkv_w_hbm, qkv_w, local_sem.at[1]),
        pltpu.make_async_copy(gain_hbm, gain, local_sem.at[6]),
        pltpu.make_async_copy(taps_hbm, taps.at[dp], local_sem.at[2]),
        pltpu.make_async_copy(cot_hbm, cot.at[pl.ds(0, frames)], local_sem.at[3]),
        pltpu.make_async_copy(out_w_hbm, out_w, local_sem.at[4]),
    ]
    barrier = pltpu.get_barrier_semaphore()
    for target in (across, *((dp, (tm + i) % 4) for i in range(1, 4))):
        pl.semaphore_signal(barrier, inc=1, device_id=target, device_id_type=MESH)
    for d in distances:
        pl.when(there(d))(
            lambda d=d: pl.semaphore_signal(
                barrier, inc=1, device_id=along_z(d), device_id_type=MESH
            )
        )
    for copy in locals_:
        copy.start()
    pl.semaphore_wait(barrier, 4 + span)

    def mine(d):
        return jnp.logical_and(there(d), (z + d + nz) % 2 == core)

    def others(d):
        return jnp.logical_and(there(d), (z + d + nz) % 2 != core)

    def slot(line, d):
        return taps.at[(z + d) * 2 + line]

    def held(d):
        return taps_hbm if d == 0 else slot(x, d)

    def z_copy(d):
        return remote(held(0), slot(x, 0), z_send.at[d + span], line_recv.at[span - d], along_z(d))

    def across_copy(d):
        return remote(held(d), slot(x, d), x_send.at[d + span], across_recv.at[d + span], across)

    def pair_copy(line, d):
        where = slot(1 - x if line else x, d)
        return remote(
            where, where, pair_send.at[line, d + span], pair_recv.at[line, d + span], pair
        )

    def line_wait(d):
        where = slot(x, d)
        remote(where, where, z_send.at[d + span], line_recv.at[d + span], pair).wait_recv()

    def across_wait(d):
        where = slot(1 - x, d)
        remote(where, where, x_send.at[d + span], across_recv.at[d + span], across).wait_recv()

    cot_copy = remote(
        cot_hbm, cot.at[pl.ds(frames, frames)], cot_send.at[0], cot_recv.at[0], (dp, tm - 1)
    )

    @pl.when(mine(0))
    def _():
        across_copy(0).start()
        for d in distances:
            start_when(there(d), lambda: z_copy(d))

    start_when(tm > 0, lambda: cot_copy)

    def pass_on(d):
        @pl.when(mine(d))
        def _():
            line_wait(d)
            across_copy(d).start()
            pair_copy(0, d).start()

    def pass_across(d):
        @pl.when(mine(d))
        def _():
            across_wait(d)
            pair_copy(1, d).start()

    def project():
        locals_[0].wait()
        locals_[1].wait()
        locals_[2].wait()
        features = clip[...].reshape(rows, width).astype(F32)
        squares = jnp.mean(features * features, axis=-1, keepdims=True)
        normed_bf = (features * lax.rsqrt(squares + 1e-06) * gain[...].reshape(1, width)).astype(BF16)
        normed[...] = normed_bf
        qkv[...] = matmul(normed_bf, qkv_w[...], PLAIN).astype(BF16)

    def attend(f):
        at = pl.ds(f * hw, hw)
        scores = matmul(qkv[at, 0:width], qkv[at, width : 2 * width], RIGHT_T) * scale
        weights = jnp.exp(scores - jnp.max(scores, axis=-1, keepdims=True))
        weights = weights / jnp.sum(weights, axis=-1, keepdims=True)
        probs[f] = weights
        weights_t[f] = weights.astype(BF16).T

    def turn():
        normed_t[...] = normed[...].T

    @pl.when(tm == 3)
    def _():
        cot[frames : 2 * frames] = jnp.zeros((frames, hw, wide), BF16)

    project()
    for d in distances[:2]:
        pass_on(d)
    attend(0)
    pass_across(0)
    for d in distances[2:4]:
        pass_on(d)
    attend(1)
    for d in distances[4:]:
        pass_on(d)
    for d in distances:
        pass_across(d)
    turn()
    for d in [0] + distances:

        @pl.when(others(d))
        def _():
            if d:
                pair_copy(0, d).wait_recv()
            pair_copy(1, d).wait_recv()

    locals_[3].wait()
    locals_[4].wait()
    locals_[5].wait()
    pl.when(tm < 3)(lambda: cot_copy.wait_recv())
    for tap in range(3):
        term = matmul(
            cot[2 - tap : 2 - tap + frames].reshape(rows, wide),
            taps[:, tap].reshape(width, wide),
            RIGHT_T,
        )
        added = term if tap == 0 else added + term
    upstream[...] = added.astype(BF16)

    own_z = pl.ds(core * zh, zh)
    owner = z // zh == core

    def rp_copy(g):
        return remote(
            grad.at[g, pl.ds((1 - core) * zh, zh)], pair_in.at[g], rp_send.at[g], rp_recv.at[g], pair
        )

    def rx_copy(g):
        return remote(x_out.at[g], x_in.at[g], rx_send.at[g], rx_recv.at[g], across)

    def rz_copy(g, d):
        return remote(
            z_out.at[g, z + d - core * zh],
            z_in.at[g, span - d],
            rz_send.at[g, span + d],
            rz_recv.at[g, span - d],
            along_z(d),
        )

    def rz_wait(g, d):
        remote(
            z_in.at[g, span + d],
            z_in.at[g, span + d],
            rz_send.at[g, span + d],
            rz_recv.at[g, span + d],
            along_z(d),
        ).wait_recv()

    def to_z(d):
        return jnp.logical_and(there(d), (z + d) // zh == core)

    def reduce_local(g):
        block = qkv_cot[:, g * width : (g + 1) * width]
        grad[g] = matmul(normed_t[...], block, PLAIN).astype(BF16).reshape(nz, 2, -1, width)
        rp_copy(g).start()

    def reduce_x(g):
        rp_copy(g).wait_recv()
        x_out[g] = (
            grad[g, own_z, 1 - x].astype(F32) + pair_in[g, :, 1 - x].astype(F32)
        ).astype(BF16)
        rx_copy(g).start()
        kept[g] = grad[g, own_z, x].astype(F32) + pair_in[g, :, x].astype(F32)

    def reduce_z(g):
        rx_copy(g).wait_recv()
        sums = kept[g] + x_in[g].astype(F32)
        kept[g] = sums
        z_out[g] = sums.astype(BF16)
        for d in reversed(distances):
            start_when(to_z(d), lambda: rz_copy(g, d))

    def reduce_end(g):
        @pl.when(owner)
        def _():
            mine = z - core * zh
            for d in distances:

                @pl.when(there(d))
                def _(d=d):
                    rz_wait(g, d)
                    kept[g, mine] = kept[g, mine] + z_in[g, span + d].astype(F32)

            slab[:, g * width : (g + 1) * width] = kept[g, mine].astype(BF16)

    def columns(t):
        return pl.ds(t * stride, window)

    mixed_cot[...] = matmul(upstream[...], out_w[...], RIGHT_T).astype(BF16)
    for f in range(frames):
        at = pl.ds(f * hw, hw)
        qkv_cot[at, 2 * width : 3 * width] = matmul(weights_t[f], mixed_cot[at, :], PLAIN).astype(
            BF16
        )
    reduce_local(2)
    for f in range(frames):
        at = pl.ds(f * hw, hw)
        p = probs[f]
        d_weights = matmul(mixed_cot[at, :], qkv[at, 2 * width : 3 * width], RIGHT_T)
        d_weights = d_weights.astype(BF16).astype(F32)
        inner = jnp.sum(p * d_weights, axis=-1, keepdims=True)
        d_scores = (p * (d_weights - inner) * scale).astype(BF16)
        qkv_cot[at, 0:width] = matmul(d_scores, qkv[at, width : 2 * width], PLAIN).astype(BF16)
        qkv_cot[at, width : 2 * width] = matmul(d_scores, qkv[at, 0:width], LEFT_T).astype(BF16)
        if f == 0:
            reduce_x(2)
    reduce_local(0)
    reduce_local(1)
    reduce_z(2)
    reduce_x(0)
    reduce_x(1)

    features = clip[...].reshape(rows, width).astype(F32)
    squares = jnp.mean(features * features, axis=-1, keepdims=True)
    root = lax.rsqrt(squares + 1e-06)
    total[...] = matmul(qkv_cot[...], qkv_w[...], RIGHT_T) * gain[...].reshape(1, width)
    reduce_z(0)
    lean = jnp.mean(features * total[...], axis=-1, keepdims=True)
    direct = root * total[...] - features * (root * root * root * lean)
    grad_in[...] = (upstream[...].astype(F32) + direct).astype(BF16).reshape(frames, hw, width)
    result_copy = pltpu.make_async_copy(grad_in, grad_in_hbm, local_sem.at[5])
    result_copy.start()
    reduce_z(1)
    pl.when(tm > 0)(lambda: cot_copy.wait_send())

    @pl.when(mine(0))
    def _():
        for d in distances:
            pl.when(there(d))(lambda: z_copy(d).wait_send())

    for d in [0] + distances:

        @pl.when(mine(d))
        def _():
            across_copy(d).wait_send()
            if d:
                pair_copy(0, d).wait_send()
            pair_copy(1, d).wait_send()

    for g in (2, 0, 1):
        reduce_end(g)

    def slab_copy(t):
        return remote(
            slab.at[:, columns(t)], slab_in.at[y], rf_send.at[t], rf_recv.at[y], (dp, t)
        )

    for t in range(4):
        start_when(jnp.logical_and(owner, tm != t), lambda: slab_copy(t))
    for source in range(2):
        local = jnp.logical_and(owner, y == source)

        @pl.when(local)
        def _():
            at = pl.ds(pl.multiple_of(tm * stride, LANES), window)
            slab_in[source] = slab[:, at]

        @pl.when(jnp.logical_not(local))
        def _():
            remote(
                slab_in.at[source], slab_in.at[source], rf_send.at[0], rf_recv.at[source], pair
            ).wait_recv()

    sums = slab_in[0].astype(F32) + slab_in[1].astype(F32)
    for t in range(4):

        @pl.when(tm == t)
        def _(t=t):
            first = t * (cols - stride)
            grad_w[...] = sums[:, first : first + cols]

    weight_copy = pltpu.make_async_copy(grad_w, grad_w_hbm, local_sem.at[7])
    weight_copy.start()

    for g in range(3):
        rp_copy(g).wait_send()
        rx_copy(g).wait_send()
        for d in distances:
            pl.when(to_z(d))(lambda: rz_copy(g, d).wait_send())
    for t in range(4):
        pl.when(jnp.logical_and(owner, tm != t))(lambda: slab_copy(t).wait_send())
    result_copy.wait()
    weight_copy.wait()


def on_device(
    ndp, ntm, clip_input, norm_gain, qkv_weight, out_weight, time_weight, upsample_cotangent
):
    _, frames, hw, width = clip_input.shape
    wide = upsample_cotangent.shape[-1]
    share = width // ndp
    fits = ndp % 4 == 0 and ndp >= 8 and ntm == 4 and frames == 2 and share % 16 == 0
    if not fits or width % LANES or wide % (2 * LANES):
        return on_device_by_collectives(
            clip_input, norm_gain, qkv_weight, out_weight, time_weight, upsample_cotangent
        )
    nz = ndp // 2
    cols = 3 * width // ntm
    window = -(-cols // LANES) * LANES
    rows = frames * hw
    steps = 2 * nz - 1
    anywhere = pl.BlockSpec(memory_space=pl.ANY)
    dma = pltpu.SemaphoreType.DMA
    grad_in, grad_w = pl.pallas_call(
        functools.partial(fused_kernel, nz),
        out_shape=(
            jax.ShapeDtypeStruct((frames, hw, width), BF16),
            jax.ShapeDtypeStruct((share, cols), F32),
        ),
        in_specs=[anywhere] * 6,
        out_specs=(anywhere, anywhere),
        scratch_shapes=[
            pltpu.VMEM((frames, hw, width), BF16),
            pltpu.VMEM((width,), F32),
            pltpu.VMEM((width, 3 * width), BF16),
            pltpu.VMEM((width, width), BF16),
            pltpu.VMEM((ndp, 3, share, wide), BF16),
            pltpu.VMEM((2 * frames, hw, wide), BF16),
            pltpu.VMEM((rows, width), BF16),
            pltpu.VMEM((width, rows), BF16),
            pltpu.VMEM((rows, 3 * width), BF16),
            pltpu.VMEM((frames, hw, hw), F32),
            pltpu.VMEM((frames, hw, hw), BF16),
            pltpu.VMEM((rows, width), F32),
            pltpu.VMEM((rows, width), BF16),
            pltpu.VMEM((rows, width), BF16),
            pltpu.VMEM((rows, 3 * width), BF16),
            pltpu.VMEM((frames, hw, width), BF16),
            pltpu.VMEM((share, cols), F32),
            pltpu.VMEM((3, nz, 2, share, width), BF16),
            pltpu.VMEM((3, nz // 2, 2, share, width), BF16),
            pltpu.VMEM((3, nz // 2, share, width), F32),
            pltpu.VMEM((3, nz // 2, share, width), BF16),
            pltpu.VMEM((3, nz // 2, share, width), BF16),
            pltpu.VMEM((3, nz // 2, share, width), BF16),
            pltpu.VMEM((3, steps, share, width), BF16),
            pltpu.VMEM((share, 3 * width), BF16),
            pltpu.VMEM((2, share, window), BF16),
            dma((8,)),
            dma((1,)),
            dma((1,)),
            dma((steps,)),
            dma((steps,)),
            dma((steps,)),
            dma((steps,)),
            dma((2, steps)),
            dma((2, steps)),
            dma((3,)),
            dma((3,)),
            dma((3,)),
            dma((3,)),
            dma((3, steps)),
            dma((3, steps)),
            dma((4,)),
            dma((2,)),
        ],
        compiler_params=pltpu.CompilerParams(
            collective_id=0, has_side_effects=True, vmem_limit_bytes=VMEM_GRANT
        ),
        cost_estimate=pl.CostEstimate(
            flops=2 * rows * width * (3 * wide + 10 * width + 6 * hw),
            bytes_accessed=4 * rows * wide + 16 * width * width,
            transcendentals=rows * hw,
        ),
    )(
        clip_input[0],
        norm_gain,
        qkv_weight,
        out_weight,
        time_weight,
        upsample_cotangent[0],
    )
    return (grad_in[None], grad_w)


def solution(mesh):
    in_specs = (
        P("dp", "tm", None, None),
        P(),
        P(),
        P(),
        P(None, "dp", None),
        P("dp", "tm", None, None),
    )
    out_specs = (P("dp", "tm", None, None), P("dp", "tm"))
    return jax.shard_map(
        functools.partial(on_device, mesh.shape["dp"], mesh.shape["tm"]),
        mesh=mesh,
        in_specs=in_specs,
        out_specs=out_specs,
        check_vma=False,
    )
```

```python
import functools
import math

import jax
import jax.numpy as jnp
from jax import lax
from jax.experimental import pallas as pl
from jax.experimental.pallas import tpu as pltpu
from jax.sharding import PartitionSpec as P


def passed_along(block, axis, distance):
    devices = range(lax.axis_size(axis))
    route = [(i - distance, i) for i in devices if i - distance in devices]
    return lax.ppermute(block, axis, route)


def rms_scaled(features, norm_gain):
    squares = jnp.mean(features * features, axis=-1, keepdims=True)
    return features * lax.rsqrt(squares + 1e-06) * norm_gain


def block_tail(qkv_rows, features, out_weight):
    width = features.shape[-1]
    queries = qkv_rows[..., :width]
    keys = qkv_rows[..., width : 2 * width]
    values = qkv_rows[..., 2 * width :]
    scores = jnp.einsum(
        "fqc,fkc->fqk", queries, keys, preferred_element_type=jnp.float32
    ) / math.sqrt(width)
    weights = jax.nn.softmax(scores, axis=-1).astype(jnp.bfloat16)
    mixed = jnp.einsum("fqk,fkc->fqc", weights, values, preferred_element_type=jnp.float32).astype(
        jnp.bfloat16
    )
    branch = jnp.einsum("fqc,cd->fqd", mixed, out_weight, preferred_element_type=jnp.float32)
    return (features + branch).astype(jnp.bfloat16)


def attention_grads(clip_rows, norm_gain, qkv_weight, out_weight, upstream):
    features = clip_rows.astype(jnp.float32)
    normed, pre_back = jax.vjp(lambda value: rms_scaled(value, norm_gain), features)
    normed_bf = normed.astype(jnp.bfloat16)
    qkv_rows = jnp.einsum(
        "fhc,cd->fhd", normed_bf, qkv_weight, preferred_element_type=jnp.float32
    ).astype(jnp.bfloat16)
    block_out, tail_back = jax.vjp(
        lambda first, second: block_tail(first, second, out_weight), qkv_rows, features
    )
    qkv_cot, feature_cot = tail_back(upstream)
    normed_cot = jnp.einsum("fhd,cd->fhc", qkv_cot, qkv_weight, preferred_element_type=jnp.float32)
    direct = pre_back(normed_cot)[0]
    input_grad = (feature_cot + direct).astype(jnp.bfloat16)
    return (input_grad, normed_bf, qkv_cot)


def on_device_by_collectives(clip_input, norm_gain, qkv_weight, out_weight, time_weight, upsample_cotangent):
    rows = clip_input[0]
    cotangent = upsample_cotangent[0]
    frames = cotangent.shape[0]
    width = rows.shape[-1]
    incoming = passed_along(cotangent, "tm", -1)
    padded = jnp.concatenate([cotangent, incoming], 0)
    piece = lax.all_gather(time_weight, "dp", axis=1, tiled=True)
    result = jnp.einsum(
        "fhd,cd->fhc", padded[2 : 2 + frames], piece[0], preferred_element_type=jnp.float32
    )
    result = result + jnp.einsum(
        "fhd,cd->fhc", padded[1 : 1 + frames], piece[1], preferred_element_type=jnp.float32
    )
    upstream = (
        result
        + jnp.einsum("fhd,cd->fhc", padded[0:frames], piece[2], preferred_element_type=jnp.float32)
    ).astype(jnp.bfloat16)
    input_grad, normed_bf, qkv_cot = attention_grads(
        rows, norm_gain, qkv_weight, out_weight, upstream
    )
    flat_normed = normed_bf.reshape(-1, width)
    flat_cot = qkv_cot.reshape(-1, 3 * width)
    shares = lax.psum_scatter(
        jnp.einsum("rc,rd->cd", flat_normed, flat_cot, preferred_element_type=jnp.float32).astype(
            jnp.bfloat16
        ),
        "dp",
        scatter_dimension=0,
        tiled=True,
    )
    qkv_grad = lax.psum_scatter(shares, "tm", scatter_dimension=1, tiled=True).astype(jnp.float32)
    return (input_grad[None], qkv_grad)


LANES = 128
VMEM_GRANT = 64 * 1024 * 1024 - 704 * 1024
MESH = pl.DeviceIdType.MESH
F32 = jnp.float32
BF16 = jnp.bfloat16
PLAIN = ((1,), (0,))
RIGHT_T = ((1,), (1,))
LEFT_T = ((0,), (0,))
CHUNKS = ((2, 1), (0, 2))


def matmul(a, b, contract):
    return lax.dot_general(a, b, (contract, ((), ())), preferred_element_type=F32)


def fused_kernel(
    nz,
    clip_hbm,
    gain_hbm,
    qkv_w_hbm,
    out_w_hbm,
    taps_hbm,
    cot_hbm,
    grad_in,
    grad_w,
    clip,
    gain,
    qkv_w,
    out_w,
    taps,
    cot,
    normed,
    normed_t,
    qkv,
    probs,
    weights_t,
    total,
    upstream,
    mixed_cot,
    qkv_cot,
    grad,
    pair_in,
    kept,
    x_out,
    x_in,
    z_out,
    z_in,
    slab,
    slab_in,
    local_sem,
    cot_send,
    cot_recv,
    z_send,
    line_recv,
    x_send,
    across_recv,
    pair_send,
    pair_recv,
    rp_send,
    rp_recv,
    rx_send,
    rx_recv,
    rz_send,
    rz_recv,
    rf_send,
    rf_recv,
):
    dp, tm = lax.axis_index("dp"), lax.axis_index("tm")
    z, x = dp // 2, dp % 2
    y, core = tm // 2, tm % 2
    frames, hw, width = clip_hbm.shape
    wide = cot_hbm.shape[-1]
    half = wide // 2
    rows = frames * hw
    cols = width * 3 // 4
    window = -(-cols // LANES) * LANES
    stride = cols // LANES * LANES
    scale = 1.0 / math.sqrt(width)
    span = nz - 1
    zh = nz // 2
    distances = [d for k in range(1, nz) for d in (-k, k)]

    across = (z * 2 + 1 - x, tm)
    pair = (dp, y * 2 + 1 - core)

    def along_z(d):
        return ((z + d) * 2 + x, tm)

    def there(d):
        return jnp.logical_and(z + d >= 0, z + d < nz)

    def remote(source, target, send, recv, device):
        return pltpu.make_async_remote_copy(
            src_ref=source,
            dst_ref=target,
            send_sem=send,
            recv_sem=recv,
            device_id=device,
            device_id_type=MESH,
        )

    def start_when(condition, copy):
        pl.when(condition)(lambda: copy().start())

    locals_ = [
        pltpu.make_async_copy(clip_hbm, clip, local_sem.at[0]),
        pltpu.make_async_copy(qkv_w_hbm, qkv_w, local_sem.at[1]),
        pltpu.make_async_copy(gain_hbm, gain, local_sem.at[6]),
        pltpu.make_async_copy(taps_hbm, taps.at[dp], local_sem.at[2]),
        pltpu.make_async_copy(cot_hbm, cot.at[pl.ds(0, frames)], local_sem.at[3]),
        pltpu.make_async_copy(out_w_hbm, out_w, local_sem.at[4]),
    ]
    barrier = pltpu.get_barrier_semaphore()
    for target in (across, *((dp, (tm + i) % 4) for i in range(1, 4))):
        pl.semaphore_signal(barrier, inc=1, device_id=target, device_id_type=MESH)
    for d in distances:
        pl.when(there(d))(
            lambda d=d: pl.semaphore_signal(
                barrier, inc=1, device_id=along_z(d), device_id_type=MESH
            )
        )
    for copy in locals_:
        copy.start()
    pl.semaphore_wait(barrier, 4 + span)

    my_half = pl.ds(pl.multiple_of(core * half, LANES), half)
    pair_half = pl.ds(pl.multiple_of((1 - core) * half, LANES), half)

    def part(c):
        return pl.ds(*CHUNKS[c])

    def slot(line, d, c):
        return taps.at[(z + d) * 2 + line, part(c), :, my_half]

    def held(d, c):
        return taps_hbm.at[part(c), :, my_half] if d == 0 else slot(x, d, c)

    def z_copy(d, c):
        return remote(
            held(0, c),
            slot(x, 0, c),
            z_send.at[d + span, c],
            line_recv.at[span - d, c],
            along_z(d),
        )

    def across_copy(d, c):
        return remote(
            held(d, c), slot(x, d, c), x_send.at[d + span, c], across_recv.at[d + span, c], across
        )

    def pair_copy(line, d, c):
        where = slot(1 - x if line else x, d, c)
        return remote(
            where, where, pair_send.at[line, d + span, c], pair_recv.at[line, d + span, c], pair
        )

    def line_wait(d, c):
        where = slot(x, d, c)
        remote(where, where, z_send.at[d + span, c], line_recv.at[d + span, c], pair).wait_recv()

    def across_wait(d, c):
        where = slot(1 - x, d, c)
        remote(
            where, where, x_send.at[d + span, c], across_recv.at[d + span, c], across
        ).wait_recv()

    def pair_wait(line, d, c):
        where = taps.at[(z + d) * 2 + (1 - x if line else x), part(c), :, pair_half]
        remote(
            where, where, pair_send.at[line, d + span, c], pair_recv.at[line, d + span, c], pair
        ).wait_recv()

    def cot_copy(f):
        return remote(cot_hbm.at[f], cot.at[frames + f], cot_send.at[f], cot_recv.at[f], (dp, tm - 1))

    for c in range(len(CHUNKS)):
        across_copy(0, c).start()
        for d in distances:
            start_when(there(d), lambda: z_copy(d, c))
    for f in range(frames):
        start_when(tm > 0, lambda: cot_copy(f))

    def pass_on(d, c):
        @pl.when(there(d))
        def _():
            line_wait(d, c)
            across_copy(d, c).start()
            pair_copy(0, d, c).start()

    def pass_across(d, c):
        @pl.when(there(d))
        def _():
            across_wait(d, c)
            pair_copy(1, d, c).start()

    def project():
        locals_[0].wait()
        locals_[1].wait()
        locals_[2].wait()
        features = clip[...].reshape(rows, width).astype(F32)
        squares = jnp.mean(features * features, axis=-1, keepdims=True)
        normed_bf = (features * lax.rsqrt(squares + 1e-06) * gain[...].reshape(1, width)).astype(BF16)
        normed[...] = normed_bf
        qkv[...] = matmul(normed_bf, qkv_w[...], PLAIN).astype(BF16)

    def attend(f):
        at = pl.ds(f * hw, hw)
        scores = matmul(qkv[at, 0:width], qkv[at, width : 2 * width], RIGHT_T) * scale
        weights = jnp.exp(scores - jnp.max(scores, axis=-1, keepdims=True))
        weights = weights / jnp.sum(weights, axis=-1, keepdims=True)
        probs[f] = weights
        weights_t[f] = weights.astype(BF16).T

    def turn():
        normed_t[...] = normed[...].T

    @pl.when(tm == 3)
    def _():
        cot[frames : 2 * frames] = jnp.zeros((frames, hw, wide), BF16)

    def add_taps(c):
        for d in [0] + distances:
            if d:
                pl.when(there(d))(lambda: pair_wait(0, d, c))
            pl.when(there(d))(lambda: pair_wait(1, d, c))
        if c == 0:
            locals_[3].wait()
            locals_[4].wait()
            locals_[5].wait()
        else:
            for f in range(frames):
                pl.when(tm < 3)(lambda: cot_copy(f).wait_recv())
        first, count = CHUNKS[c]
        added = None
        for tap in range(first, first + count):
            term = matmul(
                cot[2 - tap : 2 - tap + frames].reshape(rows, wide),
                taps[:, tap].reshape(width, wide),
                RIGHT_T,
            )
            added = term if added is None else added + term
        if c == 0:
            total[...] = added
        else:
            upstream[...] = (total[...] + added).astype(BF16)

    project()
    pass_on(-1, 0)
    pass_on(1, 0)
    attend(0)
    for d in distances[2:]:
        pass_on(d, 0)
    attend(1)
    pass_across(0, 0)
    for d in distances:
        pass_on(d, 1)
    turn()
    for d in distances:
        pass_across(d, 0)
    add_taps(0)
    for d in [0] + distances:
        pass_across(d, 1)
    add_taps(1)

    own_z = pl.ds(core * zh, zh)
    owner = z // zh == core

    def rp_copy(g):
        return remote(
            grad.at[g, pl.ds((1 - core) * zh, zh)], pair_in.at[g], rp_send.at[g], rp_recv.at[g], pair
        )

    def rx_copy(g):
        return remote(x_out.at[g], x_in.at[g], rx_send.at[g], rx_recv.at[g], across)

    def rz_copy(g, d):
        return remote(
            z_out.at[g, z + d - core * zh],
            z_in.at[g, span - d],
            rz_send.at[g, span + d],
            rz_recv.at[g, span - d],
            along_z(d),
        )

    def rz_wait(g, d):
        remote(
            z_in.at[g, span + d],
            z_in.at[g, span + d],
            rz_send.at[g, span + d],
            rz_recv.at[g, span + d],
            along_z(d),
        ).wait_recv()

    def to_z(d):
        return jnp.logical_and(there(d), (z + d) // zh == core)

    def reduce_local(g):
        block = qkv_cot[:, g * width : (g + 1) * width]
        grad[g] = matmul(normed_t[...], block, PLAIN).astype(BF16).reshape(nz, 2, -1, width)
        rp_copy(g).start()

    def reduce_x(g):
        rp_copy(g).wait_recv()
        x_out[g] = (
            grad[g, own_z, 1 - x].astype(F32) + pair_in[g, :, 1 - x].astype(F32)
        ).astype(BF16)
        rx_copy(g).start()
        kept[g] = grad[g, own_z, x].astype(F32) + pair_in[g, :, x].astype(F32)

    def reduce_z(g):
        rx_copy(g).wait_recv()
        sums = kept[g] + x_in[g].astype(F32)
        kept[g] = sums
        z_out[g] = sums.astype(BF16)
        for d in reversed(distances):
            start_when(to_z(d), lambda: rz_copy(g, d))

    def reduce_end(g):
        @pl.when(owner)
        def _():
            mine = z - core * zh
            for d in distances:

                @pl.when(there(d))
                def _(d=d):
                    rz_wait(g, d)
                    kept[g, mine] = kept[g, mine] + z_in[g, span + d].astype(F32)

            slab[:, g * width : (g + 1) * width] = kept[g, mine].astype(BF16)

    def columns(t):
        return pl.ds(t * stride, window)

    mixed_cot[...] = matmul(upstream[...], out_w[...], RIGHT_T).astype(BF16)
    for f in range(frames):
        at = pl.ds(f * hw, hw)
        qkv_cot[at, 2 * width : 3 * width] = matmul(weights_t[f], mixed_cot[at, :], PLAIN).astype(
            BF16
        )
    reduce_local(2)
    for f in range(frames):
        at = pl.ds(f * hw, hw)
        p = probs[f]
        d_weights = matmul(mixed_cot[at, :], qkv[at, 2 * width : 3 * width], RIGHT_T)
        d_weights = d_weights.astype(BF16).astype(F32)
        inner = jnp.sum(p * d_weights, axis=-1, keepdims=True)
        d_scores = (p * (d_weights - inner) * scale).astype(BF16)
        qkv_cot[at, 0:width] = matmul(d_scores, qkv[at, width : 2 * width], PLAIN).astype(BF16)
        qkv_cot[at, width : 2 * width] = matmul(d_scores, qkv[at, 0:width], LEFT_T).astype(BF16)
        if f == 0:
            reduce_x(2)
    reduce_local(0)
    reduce_local(1)
    reduce_z(2)
    reduce_x(0)
    reduce_x(1)

    features = clip[...].reshape(rows, width).astype(F32)
    squares = jnp.mean(features * features, axis=-1, keepdims=True)
    root = lax.rsqrt(squares + 1e-06)
    total[...] = matmul(qkv_cot[...], qkv_w[...], RIGHT_T) * gain[...].reshape(1, width)
    reduce_z(0)
    lean = jnp.mean(features * total[...], axis=-1, keepdims=True)
    direct = root * total[...] - features * (root * root * root * lean)
    grad_in[...] = (upstream[...].astype(F32) + direct).astype(BF16).reshape(frames, hw, width)
    reduce_z(1)
    for f in range(frames):
        pl.when(tm > 0)(lambda: cot_copy(f).wait_send())
    for c in range(len(CHUNKS)):
        across_copy(0, c).wait_send()
        pair_copy(1, 0, c).wait_send()
        for d in distances:

            @pl.when(there(d))
            def _():
                z_copy(d, c).wait_send()
                across_copy(d, c).wait_send()
                pair_copy(0, d, c).wait_send()
                pair_copy(1, d, c).wait_send()

    for g in (2, 0, 1):
        reduce_end(g)

    def slab_copy(t):
        return remote(
            slab.at[:, columns(t)], slab_in.at[y], rf_send.at[t], rf_recv.at[y], (dp, t)
        )

    for t in range(4):
        start_when(jnp.logical_and(owner, tm != t), lambda: slab_copy(t))
    for source in range(2):
        local = jnp.logical_and(owner, y == source)

        @pl.when(local)
        def _():
            at = pl.ds(pl.multiple_of(tm * stride, LANES), window)
            slab_in[source] = slab[:, at]

        @pl.when(jnp.logical_not(local))
        def _():
            remote(
                slab_in.at[source], slab_in.at[source], rf_send.at[0], rf_recv.at[source], pair
            ).wait_recv()

    sums = slab_in[0].astype(F32) + slab_in[1].astype(F32)
    for t in range(4):

        @pl.when(tm == t)
        def _(t=t):
            first = t * (cols - stride)
            grad_w[...] = sums[:, first : first + cols]

    for g in range(3):
        rp_copy(g).wait_send()
        rx_copy(g).wait_send()
        for d in distances:
            pl.when(to_z(d))(lambda: rz_copy(g, d).wait_send())
    for t in range(4):
        pl.when(jnp.logical_and(owner, tm != t))(lambda: slab_copy(t).wait_send())


def on_device(
    ndp, ntm, clip_input, norm_gain, qkv_weight, out_weight, time_weight, upsample_cotangent
):
    _, frames, hw, width = clip_input.shape
    wide = upsample_cotangent.shape[-1]
    share = width // ndp
    fits = ndp % 4 == 0 and ntm == 4 and frames == 2 and share % 16 == 0
    if not fits or width % LANES or wide % (2 * LANES):
        return on_device_by_collectives(
            clip_input, norm_gain, qkv_weight, out_weight, time_weight, upsample_cotangent
        )
    nz = ndp // 2
    cols = 3 * width // ntm
    window = -(-cols // LANES) * LANES
    rows = frames * hw
    steps = 2 * nz - 1
    chunks = len(CHUNKS)
    anywhere = pl.BlockSpec(memory_space=pl.ANY)
    dma = pltpu.SemaphoreType.DMA
    grad_in, grad_w = pl.pallas_call(
        functools.partial(fused_kernel, nz),
        out_shape=(
            pltpu.VMEM((frames, hw, width), BF16),
            pltpu.VMEM((share, cols), F32),
        ),
        in_specs=[anywhere] * 6,
        out_specs=(pl.BlockSpec(memory_space=pltpu.VMEM),) * 2,
        scratch_shapes=[
            pltpu.VMEM((frames, hw, width), BF16),
            pltpu.VMEM((width,), F32),
            pltpu.VMEM((width, 3 * width), BF16),
            pltpu.VMEM((width, width), BF16),
            pltpu.VMEM((ndp, 3, share, wide), BF16),
            pltpu.VMEM((2 * frames, hw, wide), BF16),
            pltpu.VMEM((rows, width), BF16),
            pltpu.VMEM((width, rows), BF16),
            pltpu.VMEM((rows, 3 * width), BF16),
            pltpu.VMEM((frames, hw, hw), F32),
            pltpu.VMEM((frames, hw, hw), BF16),
            pltpu.VMEM((rows, width), F32),
            pltpu.VMEM((rows, width), BF16),
            pltpu.VMEM((rows, width), BF16),
            pltpu.VMEM((rows, 3 * width), BF16),
            pltpu.VMEM((3, nz, 2, share, width), BF16),
            pltpu.VMEM((3, nz // 2, 2, share, width), BF16),
            pltpu.VMEM((3, nz // 2, share, width), F32),
            pltpu.VMEM((3, nz // 2, share, width), BF16),
            pltpu.VMEM((3, nz // 2, share, width), BF16),
            pltpu.VMEM((3, nz // 2, share, width), BF16),
            pltpu.VMEM((3, steps, share, width), BF16),
            pltpu.VMEM((share, 3 * width), BF16),
            pltpu.VMEM((2, share, window), BF16),
            dma((8,)),
            dma((2,)),
            dma((2,)),
            dma((steps, chunks)),
            dma((steps, chunks)),
            dma((steps, chunks)),
            dma((steps, chunks)),
            dma((2, steps, chunks)),
            dma((2, steps, chunks)),
            dma((3,)),
            dma((3,)),
            dma((3,)),
            dma((3,)),
            dma((3, steps)),
            dma((3, steps)),
            dma((4,)),
            dma((2,)),
        ],
        compiler_params=pltpu.CompilerParams(
            collective_id=0, has_side_effects=True, vmem_limit_bytes=VMEM_GRANT
        ),
        cost_estimate=pl.CostEstimate(
            flops=2 * rows * width * (3 * wide + 10 * width + 6 * hw),
            bytes_accessed=4 * rows * wide + 16 * width * width,
            transcendentals=rows * hw,
        ),
    )(
        clip_input[0],
        norm_gain,
        qkv_weight,
        out_weight,
        time_weight,
        upsample_cotangent[0],
    )
    return (grad_in[None], grad_w)


def solution(mesh):
    in_specs = (
        P("dp", "tm", None, None),
        P(),
        P(),
        P(),
        P(None, "dp", None),
        P("dp", "tm", None, None),
    )
    out_specs = (P("dp", "tm", None, None), P("dp", "tm"))
    return jax.shard_map(
        functools.partial(on_device, mesh.shape["dp"], mesh.shape["tm"]),
        mesh=mesh,
        in_specs=in_specs,
        out_specs=out_specs,
        check_vma=False,
    )
```
